128 devices in a mesh: lon: 64 (over y_lo, x, z, core), lat: 2 (over y_hi).
Axes of the slice: x: 4, y: 4 (y_hi: 2, y_lo: 2; y = y_hi * 2 + y_lo), z: 4, core: 2. Of those that a mesh axis runs over, the one named last changes fastest.
Arguments:
- coords: float32 [3, 1024, 128], P(None, ('lon', 'lat')), may hold values from -64 to 64, as said below
- observed: float32 [32, 1024, 128], P(None, ('lon', 'lat')), may hold values from -6 to 6
- neighbours: int32 [4, 1024], P(None, ('lon', 'lat')), may hold values from 0 to 1023, as said below
- counts: int32 [128], replicated, may hold values from 1 to 8, as said below
- lengthscale: float32 [1], replicated, may hold values from 0.3 to 1
- nugget: float32 [1], replicated, may hold values from 0.1 to 0.5
Outputs:
- predicted: float32 [32, 1024, 128], P(None, ('lon', 'lat'))
- variance: float32 [1024, 128], P(('lon', 'lat'))
The draws below stay inside these ranges and needn't reach their ends.
Inputs may be any that keep to these rules, and one draw needn't show every extreme that they name: `neighbours`: the 4 entries of a block are distinct and never the block itself. A block on band l, sub-band h, slot s names only blocks of either sub-band whose cycle position (band * 8 + slot) lies within 8 of l * 8 + s around the cycle of 512 positions. Entry l * 2 + h counts the live blocks of band l, sub-band h: its slots 0 to count - 1 are live. The entries equal to 8 are exactly those of a run of 8 consecutive bands around the cycle, both sub-bands; all others are at most 2. `coords`: point k of block b on band l, sub-band h, slot s is (r cos a, r sin a, h + w) with r = 64 / (2 pi), a = 2 pi (l + (s + u) / 8) / 64, and u, w in [0, 1).
All inputs are finite; a program needn't handle non-finite values.
Results may differ from the reference program's by a relative error of at most 0.0003.
Values sent between devices are 32-bit elements; how exact they have to be, the bound alone decides.
No kernel may reach another device: no remote copies, remote signals or barrier semaphores. Data moves between devices by JAX's collectives and lax.ppermute only.
A program may use at most 64 MiB of HBM per device.

```python
import math
import jax
import jax.numpy as jnp
from jax import lax

BS = 128
NBR = 4
NF = 32
BLK_DEV = 8
BANDS = 64
SUBS = 2
SHARDS = 128
BLOCKS = 1024


def draw_coords(key, part):
    blocks = jnp.arange(BLOCKS, dtype=jnp.int32)
    owner = blocks // BLK_DEV
    band = (owner // SUBS).astype(jnp.float32)
    sub = (owner % SUBS).astype(jnp.float32)
    slot = (blocks % BLK_DEV).astype(jnp.float32)
    first, second = jax.random.split(jax.random.fold_in(key, 11))
    along = jax.random.uniform(first, (BLOCKS, BS), jnp.float32)
    upward = jax.random.uniform(second, (BLOCKS, BS), jnp.float32)
    position = band[:, None] + (slot[:, None] + along) / BLK_DEV
    angle = 2.0 * math.pi * position / BANDS
    radius = BANDS / (2.0 * math.pi)
    height = sub[:, None] + upward
    return jnp.stack([radius * jnp.cos(angle), radius * jnp.sin(angle), height], axis=0).astype(jnp.float32)


def draw_neighbours(key, part):
    blocks = jnp.arange(BLOCKS, dtype=jnp.int32)
    owner = blocks // BLK_DEV
    band = owner // SUBS
    sub = owner % SUBS
    slot = blocks % BLK_DEV
    reach = 2 * BLK_DEV + 1
    total = reach * SUBS
    cand = jnp.arange(total, dtype=jnp.int32)
    shift = cand // SUBS - BLK_DEV
    cand_sub = cand % SUBS
    scores = jax.random.randint(jax.random.fold_in(key, 23), (BLOCKS, total), 0, 1 << 20) * total + cand[None, :]
    itself = (shift[None, :] == 0) & (cand_sub[None, :] == sub[:, None])
    ends = (shift[None, :] == BLK_DEV) | (shift[None, :] == -BLK_DEV)
    scores = jnp.where(itself | ends, -1, scores)
    best = jax.lax.top_k(scores, NBR - 2)[1].astype(jnp.int32)
    cycle = BANDS * BLK_DEV
    here = band[:, None] * BLK_DEV + slot[:, None]
    place = (here + shift[best]) % cycle
    free_pick = (place // BLK_DEV * SUBS + cand_sub[best]) * BLK_DEV + place % BLK_DEV
    forced_sub = jax.random.randint(jax.random.fold_in(key, 29), (BLOCKS, 2), 0, SUBS)
    steps = jnp.array([BLK_DEV, -BLK_DEV], dtype=jnp.int32)
    forced_place = (here + steps[None, :]) % cycle
    forced_pick = (forced_place // BLK_DEV * SUBS + forced_sub) * BLK_DEV + forced_place % BLK_DEV
    chosen = jnp.concatenate([forced_pick, free_pick], axis=1)
    return chosen.T.astype(jnp.int32)


def draw_counts(key, part):
    first, second = jax.random.split(jax.random.fold_in(key, 37))
    base = jax.random.randint(first, (SHARDS,), 1, BLK_DEV // 3 + 1)
    start = jax.random.randint(second, (), 0, BANDS)
    run = max(1, BANDS // 8)
    band = jnp.arange(SHARDS, dtype=jnp.int32) // SUBS
    heavy = (band - start) % BANDS < run
    return jnp.where(heavy, BLK_DEV, base).astype(jnp.int32)


def level_of(own_key, dims, pieces, smallest, largest):
    def one(axis_at, blocks):
        steps = jax.random.uniform(jax.random.fold_in(jax.random.fold_in(own_key, 6), axis_at), (blocks,), jnp.float32, smallest / len(pieces), largest / len(pieces))
        return jnp.repeat(jnp.exp(steps), dims[axis_at] // blocks).reshape((-1,) + (1,) * (len(dims) - axis_at - 1))

    gain = one(*pieces[0])
    for cut in pieces[1:]:
        gain = gain * one(*cut)
    return gain


def centred(key, shape, deviation, most, pieces=(), held_as=jnp.bfloat16):
    factor_of = level_of(key, shape, pieces, -0.22, 0.18) if pieces else 1.0
    values = jax.random.normal(key, shape, jnp.float32) * deviation * factor_of
    return jnp.minimum(jnp.maximum(values, -most), most).astype(held_as)


def setup_inputs(seed: int = 0) -> dict:
    splits = jax.random.split(jax.random.key(seed), 7)
    coords = draw_coords(jax.random.fold_in(splits[6], 71), 0)
    observed = centred(splits[1], (NF, BLOCKS, BS), 1.0, 6.0, ((1, 128),), jnp.float32)
    neighbours = draw_neighbours(jax.random.fold_in(splits[6], 71), 0)
    counts = draw_counts(jax.random.fold_in(splits[6], 71), 0)
    lengthscale = jnp.clip(jnp.exp(jax.random.uniform(splits[4], (1,), jnp.float32, math.log(0.3), math.log(1.0))), 0.3, 1.0)
    nugget = jnp.clip(jnp.exp(jax.random.uniform(splits[5], (1,), jnp.float32, math.log(0.1), math.log(0.5))), 0.1, 0.5)
    return {"coords": coords, "observed": observed, "neighbours": neighbours, "counts": counts, "lengthscale": lengthscale, "nugget": nugget}


def solve_group(points, values, target, scale, noise):
    count = points.shape[2]
    delta = points[:, :, :, None] - points[:, :, None, :]
    dist = jnp.sqrt(lax.optimization_barrier(jnp.sum(delta * delta, axis=1)))
    cov = jnp.exp(-dist / scale) + noise * jnp.eye(count, dtype=jnp.float32)
    factor = jnp.linalg.cholesky(cov)
    offset = points[:, :, :, None] - target[:, :, None, :]
    cross = jnp.exp(-jnp.sqrt(lax.optimization_barrier(jnp.sum(offset * offset, axis=1))) / scale)
    width = cross.shape[2]
    rhs = jnp.concatenate([cross, values], axis=2)
    solved = lax.linalg.triangular_solve(factor, rhs, left_side=True, lower=True)
    weights = solved[:, :, :width]
    projected = solved[:, :, width:]
    mean = jnp.einsum('gmb,gmf->gbf', weights, projected, precision=lax.Precision.HIGHEST)
    spread = 1.0 - lax.optimization_barrier(jnp.sum(weights * weights, axis=1))
    return (mean, spread)

def reference(coords, observed, neighbours, counts, lengthscale, nugget):
    scale = lengthscale[0]
    noise = nugget[0]
    listing = neighbours.T.astype(jnp.int32)
    group_size = 16

    def one_group(start):
        chosen = lax.dynamic_slice_in_dim(listing, start, group_size, 0).reshape(-1)
        points = jnp.take(coords, chosen, axis=1).reshape(3, group_size, NBR, BS)
        points = points.transpose(1, 0, 2, 3).reshape(group_size, 3, NBR * BS)
        values = jnp.take(observed, chosen, axis=1).reshape(NF, group_size, NBR * BS).transpose(1, 2, 0)
        target = lax.dynamic_slice_in_dim(coords, start, group_size, 1).transpose(1, 0, 2)
        return solve_group(points, values, target, scale, noise)
    starts = jnp.arange(0, BLOCKS, group_size, dtype=jnp.int32)
    means, spreads = lax.map(one_group, starts)
    mean = means.reshape(BLOCKS, BS, NF).transpose(2, 0, 1)
    spread = spreads.reshape(BLOCKS, BS)
    blocks = jnp.arange(BLOCKS, dtype=jnp.int32)
    live = blocks % BLK_DEV < counts[blocks // BLK_DEV]
    predicted = jnp.where(live[None, :, None], mean, jnp.zeros_like(mean))
    variance = jnp.where(live[:, None], spread, jnp.zeros_like(spread))
    return (predicted, variance)
```

```python
import jax
import jax.numpy as jnp
from jax import lax
from jax.experimental import pallas as pl
from jax.experimental.pallas import tpu as pltpu
from jax.sharding import PartitionSpec as P

HIGHEST = lax.Precision.HIGHEST
LEAF = 16
TASKS = 3
NBR = 4
NF = 32
W = 128
SLOTS = 8
SHIP = SLOTS - TASKS
F32 = jnp.float32

VMEM = pl.BlockSpec(memory_space=pltpu.VMEM)
SMEM = pl.BlockSpec(memory_space=pltpu.SMEM)


def params():
    return pltpu.CompilerParams(vmem_limit_bytes=40 * 2**20)


def mm(a, b):
    return lax.dot_general(
        a, b, (((1,), (0,)), ((), ())), precision=HIGHEST, preferred_element_type=F32
    )


def mmt(a, b):
    return lax.dot_general(
        a, b, (((1,), (1,)), ((), ())), precision=HIGHEST, preferred_element_type=F32
    )


def recip(p):
    r = pl.reciprocal(p, approx=True)
    r = r * (2.0 - p * r)
    return r * (2.0 - p * r)


def sweep(panel, off, rows, lanes):
    cols = [
        jnp.broadcast_to(panel[:, off + c : off + c + 1], (LEAF, W)) for c in range(LEAF)
    ]
    for i in range(LEAF):
        r = recip(jnp.broadcast_to(cols[i][i : i + 1], (LEAF, W)))
        here = rows == i
        m = jnp.where(here, 1.0 - r, cols[i] * r)
        panel = jnp.where(lanes == off + i, jnp.where(here, 1.0, 0.0), panel)
        panel = panel - m * jnp.broadcast_to(panel[i : i + 1], (LEAF, W))
        for c in range(i + 1, LEAF):
            cols[c] = cols[c] - m * jnp.broadcast_to(cols[c][i : i + 1], (LEAF, W))
    return panel


def invert(tiles):
    rows = lax.broadcasted_iota(jnp.int32, (LEAF, W), 0)
    lanes = lax.broadcasted_iota(jnp.int32, (LEAF, W), 1)
    down = lax.broadcasted_iota(jnp.int32, (W, W), 0)
    along = lax.broadcasted_iota(jnp.int32, (W, W), 1)
    for off in range(0, W, LEAF):
        swept = [sweep(t[off : off + LEAF], off, rows, lanes) for t in tiles]
        new = []
        for t, q in zip(tiles, swept):
            low, high = off, W - off - LEAF
            wide = jnp.concatenate(
                [
                    x
                    for x in (jnp.zeros((low, W), F32), q, jnp.zeros((high, W), F32))
                    if x.shape[0]
                ],
                0,
            )
            in_rows = (down >= off) & (down < off + LEAF)
            in_cols = (along >= off) & (along < off + LEAF)
            others = jnp.where(in_rows, 0.0, t)
            u = jnp.where(in_cols, 0.0, others) - mm(others, wide)
            new.append(
                jnp.concatenate(
                    [x for x in (u[:off], q, u[off + LEAF :]) if x.shape[0]], 0
                )
            )
        tiles = new
    return tiles


def pool_row(block, my_band, my_sub, bands):
    band = block // (2 * SLOTS)
    sub = (block // SLOTS) % 2
    side = (band - my_band + 1 + bands) % bands
    flip = jnp.where(sub == my_sub, 0, 1)
    return (side * 2 + flip) * SLOTS + block % SLOTS


def pack_points(bands, nb, *refs):
    pools, own, ships, pool = refs[:6], refs[6], refs[7:-1], refs[-1]
    band, sub = lax.axis_index("lon"), lax.axis_index("lat")
    for g in range(6):
        pool[:, g * SLOTS : (g + 1) * SLOTS, :] = pools[g][...]
    for s in range(SLOTS):
        dst = own.at[s] if s < TASKS else ships[s - TASKS]
        for d in range(3):
            dst[d] = jnp.zeros((8, W), F32)
        for n in range(NBR):
            row = pool_row(nb[n, s], band, sub, bands)
            dst[:, n : n + 1, :] = pool[:, pl.ds(row, 1), :]
        dst[:, NBR : NBR + 1, :] = pools[2][:, s : s + 1, :]


def pack_values(bands, nb, *refs):
    pools, own, ships, pool = refs[:6], refs[6], refs[7:-1], refs[-1]
    band, sub = lax.axis_index("lon"), lax.axis_index("lat")
    for g in range(6):
        pool[:, g * SLOTS : (g + 1) * SLOTS, :] = pools[g][...]
    for s in range(SLOTS):
        dst = own.at[s] if s < TASKS else ships[s - TASKS]
        for n in range(NBR):
            row = pool_row(nb[n, s], band, sub, bands)
            dst[n] = pool[:, pl.ds(row, 1), :].reshape(NF, W)


def for_third(counts, bands, own_third, ships, use):
    band, sub = lax.axis_index("lon"), lax.axis_index("lat")
    apart = bands // SLOTS
    for k in range(SHIP):
        giver = (band - (k + 1) * apart + bands) % bands

        @pl.when(counts[giver * 2 + sub] > TASKS - 1)
        def _():
            use(ships[k][...])

    del apart
    return band, sub


def factor(bands, counts, scale, nugget, own, *refs):
    ships, coef, var, pts, tiles, diag = refs[:SHIP], refs[SHIP], refs[SHIP + 1], *refs[SHIP + 2 :]
    pts[...] = own[...]

    def put(x):
        pts[TASKS - 1] = x

    for_third(counts, bands, None, ships, put)
    down = lax.broadcasted_iota(jnp.int32, (W, W), 0)
    along = lax.broadcasted_iota(jnp.int32, (W, W), 1)
    minus = jnp.full((W, W), -1.0, F32) / scale[0]
    noise = jnp.where(down == along, nugget[0], 0.0)
    ones = jnp.ones((8, W), F32)

    def build(s, carry):
        rows = [pts[s, d] for d in range(3)]
        cols = [r.T for r in rows]
        for a in range(NBR + 1):
            mine = [jnp.broadcast_to(c[:, a : a + 1], (W, W)) for c in cols]
            for b in range(min(a, NBR - 1) + 1):
                total = None
                for d in range(3):
                    gap = mine[d] - jnp.broadcast_to(rows[d][b : b + 1], (W, W))
                    total = gap * gap if total is None else total + gap * gap
                value = jnp.exp(jnp.sqrt(total) * minus)
                if a == b:
                    value = value + noise
                tiles[s, a, b] = value
        var[s] = ones
        return carry

    lax.fori_loop(0, TASKS, build, 0)

    def eliminate(j, carry):
        for s, g in enumerate(invert([tiles[s, j, j] for s in range(TASKS)])):
            diag[s] = g
        for at in range(NBR):

            @pl.when(j == at)
            def _():
                def one(s, inner):
                    g = diag[s]
                    d = tiles[s, at, at]
                    left = {}
                    for a in range(at + 1, NBR + 1):
                        given = tiles[s, a, at]
                        v = mm(given, g)
                        left[a] = v + mm(given - mm(v, d), g)
                    for b in range(at + 1, NBR):
                        for a in range(b, NBR + 1):
                            tiles[s, a, b] = tiles[s, a, b] - mmt(left[a], tiles[s, b, at])
                    var[s] = var[s] - mmt(ones, left[NBR] * tiles[s, NBR, at])
                    for a in range(at + 1, NBR + 1):
                        tiles[s, a, at] = left[a]
                    return inner

                lax.fori_loop(0, TASKS, one, 0)

        return carry

    lax.fori_loop(0, NBR, eliminate, 0)

    def back(s, carry):
        done = [None] * NBR
        for at in range(NBR - 1, -1, -1):
            x = tiles[s, NBR, at]
            for a in range(at + 1, NBR):
                x = x - mm(done[a], tiles[s, a, at])
            done[at] = x
            coef[s, at] = x
        return carry

    lax.fori_loop(0, TASKS, back, 0)


def combine(bands, counts, coef, var, own, *refs):
    ships, kept, sent, values = refs[:SHIP], refs[SHIP], refs[SHIP + 1], refs[SHIP + 2]
    values[...] = own[TASKS - 1]

    def put(x):
        values[...] = x

    for_third(counts, bands, None, ships, put)
    for s in range(TASKS):
        total = None
        for n in range(NBR):
            y = values[n] if s == TASKS - 1 else own[s, n]
            part = mmt(y, coef[s, n])
            total = part if total is None else total + part
        dst = sent if s == TASKS - 1 else kept.at[s]
        dst[:NF] = total
        dst[NF:] = var[s]


def assemble(bands, counts, kept, third, *refs):
    backs, predicted, variance = refs[:SHIP], refs[SHIP], refs[SHIP + 1]
    band, sub = lax.axis_index("lon"), lax.axis_index("lat")
    alive = counts[band * 2 + sub]
    for s in range(SLOTS):
        src = kept[s] if s < TASKS - 1 else third[...] if s < TASKS else backs[s - TASKS][...]
        src = jnp.where(s < alive, src, 0.0)
        predicted[:, s : s + 1, :] = src[:NF].reshape(NF, 1, W)
        variance[s : s + 1, :] = src[NF : NF + 1]


def arr(*shape):
    return jax.ShapeDtypeStruct(shape, F32)


def cost(flops, bytes_accessed):
    return pl.CostEstimate(flops=flops, bytes_accessed=bytes_accessed, transcendentals=0)


def on_device(bands, coords, observed, neighbours, counts, lengthscale, nugget):
    axes = ("lon", "lat")
    total = bands * 2
    apart = bands // SLOTS

    def shift(x, lon, flip):
        pairs = [
            (l * 2 + h, ((l + lon) % bands) * 2 + (h ^ flip))
            for l in range(bands)
            for h in range(2)
        ]
        return lax.ppermute(x, axes, pairs)

    def pool_of(x):
        return [
            x if (away, flip) == (0, 0) else shift(x, -away, flip)
            for away in (-1, 0, 1)
            for flip in (0, 1)
        ]

    def ship(parts):
        return [shift(p, (k + 1) * apart, 0) for k, p in enumerate(parts)]

    point_pool = pool_of(coords)
    value_pool = pool_of(observed)
    own_points, *out_points = pl.pallas_call(
        lambda *r: pack_points(bands, *r),
        out_shape=[arr(TASKS, 3, 8, W)] + [arr(3, 8, W)] * SHIP,
        in_specs=[SMEM] + [VMEM] * 6,
        out_specs=[VMEM] * (1 + SHIP),
        scratch_shapes=[pltpu.VMEM((3, 6 * SLOTS, W), F32)],
        compiler_params=params(),
        name="pack_points",
    )(neighbours, *point_pool)
    in_points = ship(out_points)
    own_values, *out_values = pl.pallas_call(
        lambda *r: pack_values(bands, *r),
        out_shape=[arr(TASKS, NBR, NF, W)] + [arr(NBR, NF, W)] * SHIP,
        in_specs=[SMEM] + [VMEM] * 6,
        out_specs=[VMEM] * (1 + SHIP),
        scratch_shapes=[pltpu.VMEM((NF, 6 * SLOTS, W), F32)],
        compiler_params=params(),
        name="pack_values",
    )(neighbours, *value_pool)
    in_values = ship(out_values)
    coef, var = pl.pallas_call(
        lambda *r: factor(bands, *r),
        out_shape=[arr(TASKS, NBR, W, W), arr(TASKS, 8, W)],
        in_specs=[SMEM] * 3 + [VMEM] * (1 + SHIP),
        out_specs=[VMEM] * 2,
        scratch_shapes=[
            pltpu.VMEM((TASKS, 3, 8, W), F32),
            pltpu.VMEM((TASKS, NBR + 1, NBR, W, W), F32),
            pltpu.VMEM((TASKS, W, W), F32),
        ],
        compiler_params=params(),
        cost_estimate=cost(10**10, 10**7),
        name="factor",
    )(counts, lengthscale, nugget, own_points, *in_points)
    kept, third = pl.pallas_call(
        lambda *r: combine(bands, *r),
        out_shape=[arr(TASKS - 1, NF + 8, W), arr(NF + 8, W)],
        in_specs=[SMEM] + [VMEM] * (3 + SHIP),
        out_specs=[VMEM] * 2,
        scratch_shapes=[pltpu.VMEM((NBR, NF, W), F32)],
        compiler_params=params(),
        name="combine",
    )(counts, coef, var, own_values, *in_values)
    backs = [shift(third, -(k + 1) * apart, 0) for k in range(SHIP)]
    return pl.pallas_call(
        lambda *r: assemble(bands, *r),
        out_shape=[arr(NF, SLOTS, W), arr(SLOTS, W)],
        in_specs=[SMEM] + [VMEM] * (2 + SHIP),
        out_specs=[VMEM] * 2,
        compiler_params=params(),
        name="assemble",
    )(counts, kept, third, *backs)


def solution(mesh):
    bands = mesh.shape["lon"]
    placed = (
        P(None, ("lon", "lat"), None),
        P(None, ("lon", "lat"), None),
        P(None, ("lon", "lat")),
        P(),
        P(),
        P(),
    )

    def step(*args):
        return tuple(on_device(bands, *args))

    return jax.shard_map(
        step,
        mesh=mesh,
        in_specs=placed,
        out_specs=(P(None, ("lon", "lat"), None), P(("lon", "lat"), None)),
        check_vma=False,
    )
```

```python
import jax
import jax.numpy as jnp
from jax import lax
from jax.experimental import pallas as pl
from jax.experimental.pallas import tpu as pltpu
from jax.sharding import PartitionSpec as P

HIGHEST = lax.Precision.HIGHEST
LEAF = 16
TASKS = 3
NBR = 4
NF = 32
W = 128
SLOTS = 8
SHIP = SLOTS - TASKS
ROWS = NBR * NF + 24
MASKS = (1, 3, 4, 5, 7)
F32 = jnp.float32

VMEM = pl.BlockSpec(memory_space=pltpu.VMEM)
SMEM = pl.BlockSpec(memory_space=pltpu.SMEM)


def params():
    return pltpu.CompilerParams(vmem_limit_bytes=40 * 2**20)


def mm(a, b):
    return lax.dot_general(
        a, b, (((1,), (0,)), ((), ())), precision=HIGHEST, preferred_element_type=F32
    )


def mmt(a, b):
    return lax.dot_general(
        a, b, (((1,), (1,)), ((), ())), precision=HIGHEST, preferred_element_type=F32
    )


def sweep(panel, off, rows, lanes):
    cols = [
        jnp.broadcast_to(panel[:, off + c : off + c + 1], (LEAF, W)) for c in range(LEAF)
    ]
    scale = jnp.zeros((LEAF, W), F32)
    for i in range(LEAF):
        here = rows == i
        r = jnp.broadcast_to(1.0 / cols[i][i : i + 1], (LEAF, W))
        others = jnp.where(here, 0.0, cols[i])
        scale = jnp.where(here, r, scale)
        if i + 1 < LEAF:
            ahead = others * jnp.broadcast_to(cols[i + 1][i : i + 1], (LEAF, W))
            cols[i + 1] = cols[i + 1] - r * ahead
        m = others * r
        panel = jnp.where(lanes == off + i, jnp.where(here, 1.0, 0.0), panel)
        panel = panel - m * jnp.broadcast_to(panel[i : i + 1], (LEAF, W))
        for c in range(i + 2, LEAF):
            cols[c] = cols[c] - m * jnp.broadcast_to(cols[c][i : i + 1], (LEAF, W))
    return panel * scale


def stack(*parts):
    return jnp.concatenate([x for x in parts if x.shape[0]], 0)


def invert(tiles):
    rows = lax.broadcasted_iota(jnp.int32, (LEAF, W), 0)
    lanes = lax.broadcasted_iota(jnp.int32, (LEAF, W), 1)
    along = lax.broadcasted_iota(jnp.int32, (W, W), 1)
    for off in range(0, W, LEAF):
        end = off + LEAF
        swept = [sweep(t[off:end], off, rows, lanes) for t in tiles]
        new = []
        in_cols = (along >= off) & (along < end)
        for t, q in zip(tiles, swept):
            wide = stack(jnp.zeros((off, W), F32), q, jnp.zeros((W - end, W), F32))
            base = jnp.where(in_cols, 0.0, t)

            def less(low, high, t=t, wide=wide, base=base):
                if low == high:
                    return t[low:high]
                return base[low:high] - mm(t[low:high], wide)

            soon = min(end + LEAF, W)
            new.append(stack(less(0, off), q, less(end, soon), less(soon, W)))
        tiles = new
    return tiles


def pool_row(block, my_band, my_sub, bands):
    band = block // (2 * SLOTS)
    sub = (block // SLOTS) % 2
    side = (band - my_band + 1 + bands) % bands
    flip = jnp.where(sub == my_sub, 0, 1)
    return (side * 2 + flip) * SLOTS + block % SLOTS


def pack(bands, nb, *refs):
    pools, own, ships, pool = refs[:6], refs[6], refs[7:-1], refs[-1]
    band, sub = lax.axis_index("lon"), lax.axis_index("lat")
    for g in range(6):
        pool[:, g * SLOTS : (g + 1) * SLOTS, :] = pools[g][...]
    for s in range(SLOTS):
        dst = own.at[s] if s < TASKS else ships[s - TASKS]
        dst[NBR * NF :, :] = jnp.zeros((24, W), F32)
        for n in range(NBR):
            row = pool_row(nb[n, s], band, sub, bands)
            got = pool[:, pl.ds(row, 1), :].reshape(NF + 3, W)
            dst[n * NF : (n + 1) * NF, :] = got[3:]
            for d in range(3):
                dst[NBR * NF + 8 * d + n : NBR * NF + 8 * d + n + 1, :] = got[d : d + 1]
        for d in range(3):
            at = NBR * NF + 8 * d + NBR
            dst[at : at + 1, :] = pools[2][d, s : s + 1, :]


def solve(bands, counts, scale, nugget, own, *refs):
    ships, kept, sent, work, tiles, diag = refs[:SHIP], *refs[SHIP:]
    band, sub = lax.axis_index("lon"), lax.axis_index("lat")
    apart = bands // SLOTS
    work[...] = own[...]
    for k, mask in enumerate(MASKS):

        @pl.when(counts[(band ^ (mask * apart)) * 2 + sub] > TASKS - 1)
        def _():
            work[TASKS - 1] = ships[k][...]

    down = lax.broadcasted_iota(jnp.int32, (W, W), 0)
    along = lax.broadcasted_iota(jnp.int32, (W, W), 1)
    minus = jnp.full((W, W), -1.0, F32) / scale[0]
    noise = jnp.where(down == along, nugget[0], 0.0)
    ones = jnp.ones((8, W), F32)

    def result(s):
        return sent if s == TASKS - 1 else kept.at[s]

    def build(s, carry):
        rows = [work[s, pl.ds(NBR * NF + 8 * d, 8), :] for d in range(3)]
        cols = [r.T for r in rows]
        for a in range(NBR + 1):
            mine = [jnp.broadcast_to(c[:, a : a + 1], (W, W)) for c in cols]
            for b in range(min(a, NBR - 1) + 1):
                total = None
                for d in range(3):
                    gap = mine[d] - jnp.broadcast_to(rows[d][b : b + 1], (W, W))
                    total = gap * gap if total is None else total + gap * gap
                value = jnp.exp(jnp.sqrt(total) * minus)
                if a == b:
                    value = value + noise
                tiles[s, a, b] = value
        return carry

    lax.fori_loop(0, TASKS, build, 0)
    for s in range(TASKS):
        result(s)[NF:] = jnp.ones((8, W), F32)

    def eliminate(j, carry):
        for s, g in enumerate(invert([tiles[s, j, j] for s in range(TASKS)])):
            diag[s] = g
        for at in range(NBR):

            @pl.when(j == at)
            def _():
                for s in range(TASKS):
                    g = diag[s]
                    d = tiles[s, at, at]
                    given = tiles[s, at + 1 :, at].reshape((NBR - at) * W, W)
                    left = mm(given, g)
                    left = left + mm(given - mm(left, d), g)
                    for b in range(at + 1, NBR):
                        fresh = mmt(left[(b - at - 1) * W :], tiles[s, b, at])
                        tiles[s, b:, b] = tiles[s, b:, b] - fresh.reshape(NBR + 1 - b, W, W)
                    result(s)[NF:] -= mmt(ones, left[-W:] * tiles[s, NBR, at])
                    tiles[s, at + 1 :, at] = left.reshape(NBR - at, W, W)

        return carry

    lax.fori_loop(0, NBR, eliminate, 0)
    for s in range(TASKS):
        done = [None] * NBR
        total = None
        for at in range(NBR - 1, -1, -1):
            x = tiles[s, NBR, at]
            for a in range(at + 1, NBR):
                x = x - mm(done[a], tiles[s, a, at])
            done[at] = x
            part = mmt(work[s, at * NF : (at + 1) * NF, :], x)
            total = part if total is None else total + part
        result(s)[:NF] = total


def assemble(bands, counts, kept, third, *refs):
    backs, predicted, variance = refs[:SHIP], refs[SHIP], refs[SHIP + 1]
    band, sub = lax.axis_index("lon"), lax.axis_index("lat")
    alive = counts[band * 2 + sub]
    for s in range(SLOTS):
        src = kept[s] if s < TASKS - 1 else third[...] if s < TASKS else backs[s - TASKS][...]
        src = jnp.where(s < alive, src, 0.0)
        predicted[:, s : s + 1, :] = src[:NF].reshape(NF, 1, W)
        variance[s : s + 1, :] = src[NF : NF + 1]


def arr(*shape):
    return jax.ShapeDtypeStruct(shape, F32)


def on_device(bands, coords, observed, neighbours, counts, lengthscale, nugget):
    axes = ("lon", "lat")
    total = bands * 2
    apart = bands // SLOTS

    def shift(x, lon, flip):
        pairs = [
            (l * 2 + h, ((l + lon) % bands) * 2 + (h ^ flip))
            for l in range(bands)
            for h in range(2)
        ]
        return lax.ppermute(x, axes, pairs)

    def pool_of(x):
        return [
            x if (away, flip) == (0, 0) else shift(x, -away, flip)
            for away in (-1, 0, 1)
            for flip in (0, 1)
        ]

    def trade(x, mask):
        pairs = [
            (l * 2 + h, (l ^ (mask * apart)) * 2 + h) for l in range(bands) for h in range(2)
        ]
        return lax.ppermute(x, axes, pairs)

    pool = pool_of(jnp.concatenate([coords, observed], axis=0))
    own, *out = pl.pallas_call(
        lambda *r: pack(bands, *r),
        out_shape=[arr(TASKS, ROWS, W)] + [arr(ROWS, W)] * SHIP,
        in_specs=[SMEM] + [VMEM] * 6,
        out_specs=[VMEM] * (1 + SHIP),
        scratch_shapes=[pltpu.VMEM((NF + 3, 6 * SLOTS, W), F32)],
        compiler_params=params(),
        name="pack",
    )(neighbours, *pool)
    ships = [trade(x, mask) for x, mask in zip(out, MASKS)]
    kept, third = pl.pallas_call(
        lambda *r: solve(bands, *r),
        out_shape=[arr(TASKS - 1, NF + 8, W), arr(NF + 8, W)],
        in_specs=[SMEM] * 3 + [VMEM] * (1 + SHIP),
        out_specs=[VMEM] * 2,
        scratch_shapes=[
            pltpu.VMEM((TASKS, ROWS, W), F32),
            pltpu.VMEM((TASKS, NBR + 1, NBR, W, W), F32),
            pltpu.VMEM((TASKS, W, W), F32),
        ],
        compiler_params=params(),
        name="solve",
    )(counts, lengthscale, nugget, own, *ships)
    backs = [trade(third, mask) for mask in MASKS]
    return pl.pallas_call(
        lambda *r: assemble(bands, *r),
        out_shape=[arr(NF, SLOTS, W), arr(SLOTS, W)],
        in_specs=[SMEM] + [VMEM] * (2 + SHIP),
        out_specs=[VMEM] * 2,
        compiler_params=params(),
        name="assemble",
    )(counts, kept, third, *backs)


def solution(mesh):
    bands = mesh.shape["lon"]
    placed = (
        P(None, ("lon", "lat"), None),
        P(None, ("lon", "lat"), None),
        P(None, ("lon", "lat")),
        P(),
        P(),
        P(),
    )

    def step(*args):
        return tuple(on_device(bands, *args))

    return jax.shard_map(
        step,
        mesh=mesh,
        in_specs=placed,
        out_specs=(P(None, ("lon", "lat"), None), P(("lon", "lat"), None)),
        check_vma=False,
    )
```

```python
import functools

import jax
import jax.numpy as jnp
from jax import lax
from jax.experimental import pallas as pl
from jax.experimental.pallas import tpu as pltpu
from jax.sharding import PartitionSpec as P

HIGHEST = lax.Precision.HIGHEST
LEAF = 16
TASKS = 3
NBR = 4
NF = 32
W = 128
SLOTS = 8
SHIP = SLOTS - TASKS
ROWS = NBR * NF + 24
MASKS = (1, 3, 4, 5, 7)
F32 = jnp.float32

VMEM = pl.BlockSpec(memory_space=pltpu.VMEM)
SMEM = pl.BlockSpec(memory_space=pltpu.SMEM)


def params():
    return pltpu.CompilerParams(vmem_limit_bytes=40 * 2**20)


def mm(a, b):
    return lax.dot_general(
        a, b, (((1,), (0,)), ((), ())), precision=HIGHEST, preferred_element_type=F32
    )


def mmt(a, b):
    return lax.dot_general(
        a, b, (((1,), (1,)), ((), ())), precision=HIGHEST, preferred_element_type=F32
    )


def halves(a):
    high = a.astype(jnp.bfloat16)
    return high, (a - high.astype(F32)).astype(jnp.bfloat16)


def mm1(a, b):
    return lax.dot_general(
        a.astype(jnp.bfloat16),
        b.astype(jnp.bfloat16),
        (((1,), (0,)), ((), ())),
        preferred_element_type=F32,
    )


def mm3(a, b):
    (ah, al), (bh, bl) = halves(a), halves(b)
    return mm1(ah, bh) + (mm1(ah, bl) + mm1(al, bh))


def stack(*parts):
    return jnp.concatenate([x for x in parts if x.shape[0]], 0)


def sweeps(panels, off, tick):
    half = LEAF // 2
    down = lax.broadcasted_iota(jnp.int32, (half, W), 0)
    lane = lax.broadcasted_iota(jnp.int32, (half, W), 1)
    pairs = [[p[:half], p[half:]] for p in panels]

    def spread(x, at):
        return [jnp.broadcast_to(x[:, at + c : at + c + 1], (half, W)) for c in range(half)]

    for h in range(2):
        at = off + half * h
        inside = (lane >= at) & (lane < at + half)
        cols = [spread(p[h], at) for p in pairs]
        far = [spread(p[1 - h], at) for p in pairs]
        mine = [jnp.where(inside, jnp.where(lane == down + at, 1.0, 0.0), p[h]) for p in pairs]
        for i in range(0, half, 2):
            for s, col in enumerate(cols):
                p, q, r = (
                    jnp.broadcast_to(col[c][k : k + 1], (half, W))
                    for c, k in ((i, i), (i + 1, i), (i + 1, i + 1))
                )
                over = 1.0 / (p * r - q * q)
                x = jnp.where(down == i, col[i] - 1.0, col[i])
                y = jnp.where(down == i + 1, col[i + 1] - 1.0, col[i + 1])
                x, y = r * x - q * y, p * y - q * x
                for c in range(i + 2, min(i + 4, half)):
                    ahead = x * jnp.broadcast_to(col[c][i : i + 1], (half, W)) + y * jnp.broadcast_to(
                        col[c][i + 1 : i + 2], (half, W)
                    )
                    col[c] = col[c] - over * ahead
                x, y = over * x, over * y
                mine[s] = mine[s] - (
                    x * jnp.broadcast_to(mine[s][i : i + 1], (half, W))
                    + y * jnp.broadcast_to(mine[s][i + 1 : i + 2], (half, W))
                )
                for c in range(i + 4, half):
                    col[c] = col[c] - (
                        x * jnp.broadcast_to(col[c][i : i + 1], (half, W))
                        + y * jnp.broadcast_to(col[c][i + 1 : i + 2], (half, W))
                    )
            tick()
            tick()
        for s, p in enumerate(pairs):
            own = mine[s]
            gone = total_of(
                [far[s][c] * jnp.broadcast_to(own[c : c + 1], (half, W)) for c in range(half)]
            )
            p[h], p[1 - h] = own, jnp.where(inside, 0.0, p[1 - h]) - gone
    return [jnp.concatenate(p, 0) for p in pairs]


def total_of(terms):
    while len(terms) > 1:
        terms = [sum(terms[k : k + 2][1:], terms[k]) for k in range(0, len(terms), 2)]
    return terms[0]


def outer(column, q, off):
    return total_of(
        [
            jnp.broadcast_to(column[:, off + c : off + c + 1], (LEAF, W))
            * jnp.broadcast_to(q[c : c + 1], (LEAF, W))
            for c in range(LEAF)
        ]
    )


def invert(tiles, behind):
    along = lax.broadcasted_iota(jnp.int32, (W, W), 1)
    state = {"ticks": 0, "done": 0}

    def tick():
        state["ticks"] += 1
        while state["done"] * W < state["ticks"] * len(behind):
            behind[state["done"]]()
            state["done"] += 1

    for off in range(0, W, LEAF):
        end = off + LEAF
        swept = sweeps([t[off:end] for t in tiles], off, tick)
        new = []
        in_cols = (along >= off) & (along < end)
        for t, q in zip(tiles, swept):
            wide = stack(jnp.zeros((off, W), F32), q, jnp.zeros((W - end, W), F32))
            u = jnp.where(in_cols, 0.0, t) - mm(t, wide)
            soon = min(end + LEAF, W)
            parts = [u[:off], q]
            if soon > end:
                parts.append(
                    jnp.where(in_cols[:LEAF], 0.0, t[end:soon]) - outer(t[end:soon], q, off)
                )
            new.append(stack(*parts, u[soon:]))
        tiles = new
    return tiles


def pool_row(block, my_band, my_sub, bands):
    band = block // (2 * SLOTS)
    sub = (block // SLOTS) % 2
    side = (band - my_band + 1 + bands) % bands
    flip = jnp.where(sub == my_sub, 0, 1)
    return (side * 2 + flip) * SLOTS + block % SLOTS


def pack(bands, nb, *refs):
    pools, own, ships, pool = refs[:6], refs[6], refs[7:-1], refs[-1]
    band, sub = lax.axis_index("lon"), lax.axis_index("lat")
    for g in range(6):
        pool[:, g * SLOTS : (g + 1) * SLOTS, :] = pools[g][...]
    for s in range(SLOTS):
        dst = own.at[s] if s < TASKS else ships[s - TASKS]
        dst[NBR * NF :, :] = jnp.zeros((24, W), F32)
        for n in range(NBR):
            row = pool_row(nb[n, s], band, sub, bands)
            got = pool[:, pl.ds(row, 1), :].reshape(NF + 3, W)
            dst[n * NF : (n + 1) * NF, :] = got[3:]
            for d in range(3):
                dst[NBR * NF + 8 * d + n : NBR * NF + 8 * d + n + 1, :] = got[d : d + 1]
        for d in range(3):
            at = NBR * NF + 8 * d + NBR
            dst[at : at + 1, :] = pools[2][d, s : s + 1, :]


def solve(bands, counts, scale, nugget, own, *refs):
    ships, kept, sent, work, tiles, diag, left = refs[:SHIP], *refs[SHIP:]
    band, sub = lax.axis_index("lon"), lax.axis_index("lat")
    apart = bands // SLOTS
    work[...] = own[...]
    for k, mask in enumerate(MASKS):

        @pl.when(counts[(band ^ (mask * apart)) * 2 + sub] > TASKS - 1)
        def _():
            work[TASKS - 1] = ships[k][...]

    down = lax.broadcasted_iota(jnp.int32, (W, W), 0)
    along = lax.broadcasted_iota(jnp.int32, (W, W), 1)
    minus = jnp.full((W, W), -1.4426950408889634, F32) / scale[0]
    noise = jnp.where(down == along, nugget[0], 0.0)
    ones = jnp.ones((8, W), F32)

    def result(s):
        return sent if s == TASKS - 1 else kept.at[s]

    points = {}

    def build(s, a, b):
        if s not in points:
            rows = [work[s, NBR * NF + 8 * d : NBR * NF + 8 * d + 8, :] for d in range(3)]
            points[s] = rows, [r.T for r in rows]
        rows, cols = points[s]
        total = None
        for d in range(3):
            gap = jnp.broadcast_to(cols[d][:, a : a + 1], (W, W)) - jnp.broadcast_to(
                rows[d][b : b + 1], (W, W)
            )
            total = gap * gap if total is None else total + gap * gap
        value = jnp.exp2(total * lax.rsqrt(jnp.maximum(total, 1e-30)) * minus)
        tiles[s, a, b] = value + noise if a == b else value

    def rows_of(s, b, low):
        return stack(
            tiles[s, low:, b].reshape((NBR + 1 - low) * W, W), work[s, b * NF : (b + 1) * NF, :]
        )

    def factor(s, j, given):
        g = diag[j % 2, s]
        left = mm3(given, g)
        return left + mm3(given - mm(left, tiles[s, j, j]), g)

    def near(s, j):
        v = factor(s, j, tiles[s, j + 1, j])
        tiles[s, j + 1, j + 1] -= mmt(v, tiles[s, j + 1, j])

    def rest(s, j):
        low = j + 2 if j + 1 < NBR else NBR
        given = rows_of(s, j, low)
        v = factor(s, j, given)
        left[s, : v.shape[0]] = v
        result(s)[NF:] -= mmt(ones, v[-W - NF : -NF] * tiles[s, NBR, j])
        result(s)[:NF] += mmt(v[-NF:], tiles[s, NBR, j])

    def update(s, j, b):
        low = max(b, j + 2)
        size = (NBR + 1 - low) * W
        start = (low - (j + 2)) * W
        fresh = mmt(left[s, start : start + size + NF], tiles[s, b, j])
        tiles[s, low:, b] -= fresh[:size].reshape(NBR + 1 - low, W, W)
        work[s, b * NF : (b + 1) * NF, :] -= fresh[size:]

    tasks = range(TASKS)
    for s in tasks:
        result(s)[:NF] = jnp.zeros((NF, W), F32)
        result(s)[NF:] = ones
        build(s, 0, 0)
    behind = [
        functools.partial(build, s, a, b)
        for a in range(1, NBR + 1)
        for s in tasks
        for b in range(min(a, NBR - 1) + 1)
    ]
    for j in range(NBR):
        for s, g in enumerate(invert([tiles[s, j, j] for s in tasks], behind)):
            diag[j % 2, s] = g
        if j + 1 < NBR:
            for s in tasks:
                near(s, j)
            behind = [functools.partial(rest, s, j) for s in tasks]
            behind += [functools.partial(update, s, j, b) for b in range(j + 1, NBR) for s in tasks]
        else:
            for s in tasks:
                rest(s, j)


def assemble(bands, counts, kept, third, *refs):
    backs, predicted, variance = refs[:SHIP], refs[SHIP], refs[SHIP + 1]
    band, sub = lax.axis_index("lon"), lax.axis_index("lat")
    alive = counts[band * 2 + sub]
    for s in range(SLOTS):
        src = kept[s] if s < TASKS - 1 else third[...] if s < TASKS else backs[s - TASKS][...]
        src = jnp.where(s < alive, src, 0.0)
        predicted[:, s : s + 1, :] = src[:NF].reshape(NF, 1, W)
        variance[s : s + 1, :] = src[NF : NF + 1]


def arr(*shape):
    return jax.ShapeDtypeStruct(shape, F32)


def on_device(bands, coords, observed, neighbours, counts, lengthscale, nugget):
    axes = ("lon", "lat")
    total = bands * 2
    apart = bands // SLOTS

    def shift(x, lon, flip):
        pairs = [
            (l * 2 + h, ((l + lon) % bands) * 2 + (h ^ flip))
            for l in range(bands)
            for h in range(2)
        ]
        return lax.ppermute(x, axes, pairs)

    def pool_of(x):
        return [
            x if (away, flip) == (0, 0) else shift(x, -away, flip)
            for away in (-1, 0, 1)
            for flip in (0, 1)
        ]

    def trade(x, mask):
        pairs = [
            (l * 2 + h, (l ^ (mask * apart)) * 2 + h) for l in range(bands) for h in range(2)
        ]
        return lax.ppermute(x, axes, pairs)

    pool = pool_of(jnp.concatenate([coords, observed], axis=0))
    own, *out = pl.pallas_call(
        lambda *r: pack(bands, *r),
        out_shape=[arr(TASKS, ROWS, W)] + [arr(ROWS, W)] * SHIP,
        in_specs=[SMEM] + [VMEM] * 6,
        out_specs=[VMEM] * (1 + SHIP),
        scratch_shapes=[pltpu.VMEM((NF + 3, 6 * SLOTS, W), F32)],
        compiler_params=params(),
        name="pack",
    )(neighbours, *pool)
    ships = [trade(x, mask) for x, mask in zip(out, MASKS)]
    kept, third = pl.pallas_call(
        lambda *r: solve(bands, *r),
        out_shape=[arr(TASKS - 1, NF + 8, W), arr(NF + 8, W)],
        in_specs=[SMEM] * 3 + [VMEM] * (1 + SHIP),
        out_specs=[VMEM] * 2,
        scratch_shapes=[
            pltpu.VMEM((TASKS, ROWS, W), F32),
            pltpu.VMEM((TASKS, NBR + 1, NBR, W, W), F32),
            pltpu.VMEM((2, TASKS, W, W), F32),
            pltpu.VMEM((TASKS, (NBR - 1) * W + NF, W), F32),
        ],
        compiler_params=params(),
        name="solve",
    )(counts, lengthscale, nugget, own, *ships)
    backs = [trade(third, mask) for mask in MASKS]
    return pl.pallas_call(
        lambda *r: assemble(bands, *r),
        out_shape=[arr(NF, SLOTS, W), arr(SLOTS, W)],
        in_specs=[SMEM] + [VMEM] * (2 + SHIP),
        out_specs=[VMEM] * 2,
        compiler_params=params(),
        name="assemble",
    )(counts, kept, third, *backs)


def solution(mesh):
    bands = mesh.shape["lon"]
    placed = (
        P(None, ("lon", "lat"), None),
        P(None, ("lon", "lat"), None),
        P(None, ("lon", "lat")),
        P(),
        P(),
        P(),
    )

    def step(*args):
        return tuple(on_device(bands, *args))

    return jax.shard_map(
        step,
        mesh=mesh,
        in_specs=placed,
        out_specs=(P(None, ("lon", "lat"), None), P(("lon", "lat"), None)),
        check_vma=False,
    )
```

```python
import functools

import jax
import jax.numpy as jnp
from jax import lax
from jax.experimental import pallas as pl
from jax.experimental.pallas import tpu as pltpu
from jax.sharding import PartitionSpec as P

LEAF = 16
TASKS = 3
NBR = 4
NF = 32
W = 128
SLOTS = 8
SHIP = SLOTS - TASKS
ROWS = NBR * NF + 24
MASKS = (7, 5, 4, 3, 1)
F32 = jnp.float32

VMEM = pl.BlockSpec(memory_space=pltpu.VMEM)
SMEM = pl.BlockSpec(memory_space=pltpu.SMEM)


def params():
    return pltpu.CompilerParams(vmem_limit_bytes=40 * 2**20)


BF16 = jnp.bfloat16


def dot(a, b, across):
    return lax.dot_general(
        a, b, (((1,), (1 if across else 0,)), ((), ())), preferred_element_type=F32
    )


def thirds(a):
    high = a.astype(BF16)
    gap = a - high.astype(F32)
    middle = gap.astype(BF16)
    return high, middle, (gap - middle.astype(F32)).astype(BF16)


def halves(a):
    high = a.astype(BF16)
    return high, (a - high.astype(F32)).astype(BF16)


def six(a, b, across):
    a1, a2, a3 = a
    b1, b2, b3 = b
    return dot(
        jnp.concatenate([a3, a1, a2, a2, a1, a1], 1),
        jnp.concatenate([b1, b3, b2, b1, b2, b1], 1 if across else 0),
        across,
    )


def turned(a, b):
    a1, a2, a3 = thirds(a)
    b1, b2, b3 = thirds(b)
    return lax.dot_general(
        jnp.concatenate([a3, a1, a2, a2, a1, a1], 0),
        jnp.concatenate([b1, b3, b2, b1, b2, b1], 0),
        (((0,), (0,)), ((), ())),
        preferred_element_type=F32,
    )


def mm(a, b):
    return six(thirds(a), thirds(b), False)


def mmt(a, b):
    return six(thirds(a), thirds(b), True)


def mm3(a, b):
    (a1, a2), (b1, b2) = halves(a), halves(b)
    return dot(jnp.concatenate([a2, a1, a1], 1), jnp.concatenate([b1, b2, b1], 0), False)


def stack(*parts):
    return jnp.concatenate([x for x in parts if x.shape[0]], 0)


def sweeps(panels, off, tick):
    half = LEAF // 2
    down = lax.broadcasted_iota(jnp.int32, (half, W), 0)
    lane = lax.broadcasted_iota(jnp.int32, (half, W), 1)
    pairs = [[p[:half], p[half:]] for p in panels]

    def spread(x, at):
        return [jnp.broadcast_to(x[:, at + c : at + c + 1], (half, W)) for c in range(half)]

    for h in range(2):
        at = off + half * h
        inside = (lane >= at) & (lane < at + half)
        cols = [spread(p[h], at) for p in pairs]
        far = [spread(p[1 - h], at) for p in pairs]
        mine = [jnp.where(inside, jnp.where(lane == down + at, 1.0, 0.0), p[h]) for p in pairs]
        for i in range(0, half, 2):
            for s, col in enumerate(cols):
                p, q, r = (
                    jnp.broadcast_to(col[c][k : k + 1], (half, W))
                    for c, k in ((i, i), (i + 1, i), (i + 1, i + 1))
                )
                over = 1.0 / (p * r - q * q)
                x = jnp.where(down == i, col[i] - 1.0, col[i])
                y = jnp.where(down == i + 1, col[i + 1] - 1.0, col[i + 1])
                x, y = r * x - q * y, p * y - q * x
                for c in range(i + 2, min(i + 4, half)):
                    ahead = x * jnp.broadcast_to(col[c][i : i + 1], (half, W)) + y * jnp.broadcast_to(
                        col[c][i + 1 : i + 2], (half, W)
                    )
                    col[c] = col[c] - over * ahead
                x, y = over * x, over * y
                mine[s] = mine[s] - (
                    x * jnp.broadcast_to(mine[s][i : i + 1], (half, W))
                    + y * jnp.broadcast_to(mine[s][i + 1 : i + 2], (half, W))
                )
                for c in range(i + 4, half):
                    col[c] = col[c] - (
                        x * jnp.broadcast_to(col[c][i : i + 1], (half, W))
                        + y * jnp.broadcast_to(col[c][i + 1 : i + 2], (half, W))
                    )
            tick()
            tick()
        for s, p in enumerate(pairs):
            own = mine[s]
            gone = total_of(
                [far[s][c] * jnp.broadcast_to(own[c : c + 1], (half, W)) for c in range(half)]
            )
            p[h], p[1 - h] = own, jnp.where(inside, 0.0, p[1 - h]) - gone
    return [jnp.concatenate(p, 0) for p in pairs]


def total_of(terms):
    while len(terms) > 1:
        terms = [sum(terms[k : k + 2][1:], terms[k]) for k in range(0, len(terms), 2)]
    return terms[0]


def invert(tiles, behind):
    along = lax.broadcasted_iota(jnp.int32, (W, W), 1)
    state = {"ticks": 0, "done": 0}

    def tick():
        state["ticks"] += 1
        while state["done"] * W < state["ticks"] * len(behind):
            behind[state["done"]]()
            state["done"] += 1

    for off in range(0, W, LEAF):
        end = off + LEAF
        swept = sweeps([t[off:end] for t in tiles], off, tick)
        new = []
        in_cols = (along >= off) & (along < end)
        swept_lanes = along[:LEAF] < off
        for t, q in zip(tiles, swept):
            u = jnp.where(in_cols, 0.0, t) - turned(jnp.where(swept_lanes, -t[off:end], t[off:end]), q)
            new.append(stack(u[:off], q, u[end:]))
        tiles = new
    return tiles


def pool_row(block, my_band, my_sub, bands):
    band = block // (2 * SLOTS)
    sub = (block // SLOTS) % 2
    side = (band - my_band + 1 + bands) % bands
    flip = jnp.where(sub == my_sub, 0, 1)
    return (side * 2 + flip) * SLOTS + block % SLOTS


def pack(bands, nb, *refs):
    pools, own, ships, pool = refs[:6], refs[6], refs[7:-1], refs[-1]
    band, sub = lax.axis_index("lon"), lax.axis_index("lat")
    for g in range(6):
        pool[:, g * SLOTS : (g + 1) * SLOTS, :] = pools[g][...]
    for s in range(SLOTS):
        dst = own.at[s] if s < TASKS else ships[s - TASKS]
        dst[NBR * NF :, :] = jnp.zeros((24, W), F32)
        for n in range(NBR):
            row = pool_row(nb[n, s], band, sub, bands)
            got = pool[:, pl.ds(row, 1), :].reshape(NF + 3, W)
            dst[n * NF : (n + 1) * NF, :] = got[3:]
            for d in range(3):
                dst[NBR * NF + 8 * d + n : NBR * NF + 8 * d + n + 1, :] = got[d : d + 1]
        for d in range(3):
            at = NBR * NF + 8 * d + NBR
            dst[at : at + 1, :] = pools[2][d, s : s + 1, :]


def solve(bands, counts, scale, nugget, own, *refs):
    ships, kept, sent, work, tiles, diag, left = refs[:SHIP], *refs[SHIP:]
    band, sub = lax.axis_index("lon"), lax.axis_index("lat")
    apart = bands // SLOTS
    work[...] = own[...]
    for k, mask in enumerate(MASKS):

        @pl.when(counts[(band ^ (mask * apart)) * 2 + sub] > TASKS - 1)
        def _():
            work[TASKS - 1] = ships[k][...]

    down = lax.broadcasted_iota(jnp.int32, (W, W), 0)
    along = lax.broadcasted_iota(jnp.int32, (W, W), 1)
    minus = jnp.full((W, W), -1.4426950408889634, F32) / scale[0]
    noise = jnp.where(down == along, nugget[0], 0.0)
    ones = jnp.ones((8, W), F32)

    def result(s):
        return sent if s == TASKS - 1 else kept.at[s]

    points = {}

    def build(s, a):
        if s not in points:
            rows = [work[s, NBR * NF + 8 * d : NBR * NF + 8 * d + 8, :] for d in range(3)]
            points[s] = rows, [r.T for r in rows]
        rows, cols = points[s]
        mine = [jnp.broadcast_to(c[:, a : a + 1], (W, W)) for c in cols]
        for b in range(min(a, NBR - 1) + 1):
            total = None
            for d in range(3):
                gap = mine[d] - jnp.broadcast_to(rows[d][b : b + 1], (W, W))
                total = gap * gap if total is None else total + gap * gap
            value = jnp.exp2(total * lax.rsqrt(jnp.maximum(total, 1e-30)) * minus)
            tiles[s, a, b] = value + noise if a == b else value

    def rows_of(s, b, low):
        return stack(
            tiles[s, low:, b].reshape((NBR + 1 - low) * W, W), work[s, b * NF : (b + 1) * NF, :]
        )

    def factor(s, j, given):
        g = diag[j % 2, s]
        left = mm3(given, g)
        return left + mm3(given - mm(left, tiles[s, j, j]), g)

    def near(s, j):
        v = factor(s, j, tiles[s, j + 1, j])
        tiles[s, j + 1, j + 1] -= mmt(v, tiles[s, j + 1, j])

    def rest(s, j):
        low = j + 2 if j + 1 < NBR else NBR
        given = rows_of(s, j, low)
        v = factor(s, j, given)
        left[s, : v.shape[0]] = v
        result(s)[NF:] -= mmt(ones, v[-W - NF : -NF] * tiles[s, NBR, j])
        result(s)[:NF] += mmt(v[-NF:], tiles[s, NBR, j])

    def update(s, j, b):
        low = max(b, j + 2)
        size = (NBR + 1 - low) * W
        start = (low - (j + 2)) * W
        fresh = mmt(left[s, start : start + size + NF], tiles[s, b, j])
        tiles[s, low:, b] -= fresh[:size].reshape(NBR + 1 - low, W, W)
        work[s, b * NF : (b + 1) * NF, :] -= fresh[size:]

    tasks = range(TASKS)
    for s in tasks:
        result(s)[:NF] = jnp.zeros((NF, W), F32)
        result(s)[NF:] = ones
        build(s, 0)
    behind = [functools.partial(build, s, a) for a in range(1, NBR + 1) for s in tasks]
    for j in range(NBR):
        for s, g in enumerate(invert([tiles[s, j, j] for s in tasks], behind)):
            diag[j % 2, s] = g
        if j + 1 < NBR:
            for s in tasks:
                near(s, j)
            behind = [functools.partial(rest, s, j) for s in tasks]
            behind += [functools.partial(update, s, j, b) for b in range(j + 1, NBR) for s in tasks]
        else:
            for s in tasks:
                rest(s, j)


def assemble(bands, counts, kept, third, *refs):
    backs, predicted, variance = refs[:SHIP], refs[SHIP], refs[SHIP + 1]
    band, sub = lax.axis_index("lon"), lax.axis_index("lat")
    alive = counts[band * 2 + sub]
    for s in range(SLOTS):
        src = kept[s] if s < TASKS - 1 else third[...] if s < TASKS else backs[s - TASKS][...]
        src = jnp.where(s < alive, src, 0.0)
        predicted[:, s : s + 1, :] = src[:NF].reshape(NF, 1, W)
        variance[s : s + 1, :] = src[NF : NF + 1]


def arr(*shape):
    return jax.ShapeDtypeStruct(shape, F32)


def on_device(bands, coords, observed, neighbours, counts, lengthscale, nugget):
    axes = ("lon", "lat")
    total = bands * 2
    apart = bands // SLOTS

    def shift(x, lon, flip):
        pairs = [
            (l * 2 + h, ((l + lon) % bands) * 2 + (h ^ flip))
            for l in range(bands)
            for h in range(2)
        ]
        return lax.ppermute(x, axes, pairs)

    def pool_of(x):
        other = shift(x, 0, 1)
        before, after = shift(x, 1, 0), shift(x, -1, 0)
        return [before, shift(other, 1, 0), x, other, after, shift(other, -1, 0)]

    def trade(x, mask):
        pairs = [
            (l * 2 + h, (l ^ (mask * apart)) * 2 + h) for l in range(bands) for h in range(2)
        ]
        return lax.ppermute(x, axes, pairs)

    pool = pool_of(jnp.concatenate([coords, observed], axis=0))
    own, *out = pl.pallas_call(
        lambda *r: pack(bands, *r),
        out_shape=[arr(TASKS, ROWS, W)] + [arr(ROWS, W)] * SHIP,
        in_specs=[SMEM] + [VMEM] * 6,
        out_specs=[VMEM] * (1 + SHIP),
        scratch_shapes=[pltpu.VMEM((NF + 3, 6 * SLOTS, W), F32)],
        compiler_params=params(),
        name="pack",
    )(neighbours, *pool)
    ships = [trade(x, mask) for x, mask in zip(out, MASKS)]
    kept, third = pl.pallas_call(
        lambda *r: solve(bands, *r),
        out_shape=[arr(TASKS - 1, NF + 8, W), arr(NF + 8, W)],
        in_specs=[SMEM] * 3 + [VMEM] * (1 + SHIP),
        out_specs=[VMEM] * 2,
        scratch_shapes=[
            pltpu.VMEM((TASKS, ROWS, W), F32),
            pltpu.VMEM((TASKS, NBR + 1, NBR, W, W), F32),
            pltpu.VMEM((2, TASKS, W, W), F32),
            pltpu.VMEM((TASKS, (NBR - 1) * W + NF, W), F32),
        ],
        compiler_params=params(),
        name="solve",
    )(counts, lengthscale, nugget, own, *ships)
    backs = [trade(third, mask) for mask in MASKS]
    return pl.pallas_call(
        lambda *r: assemble(bands, *r),
        out_shape=[arr(NF, SLOTS, W), arr(SLOTS, W)],
        in_specs=[SMEM] + [VMEM] * (2 + SHIP),
        out_specs=[VMEM] * 2,
        compiler_params=params(),
        name="assemble",
    )(counts, kept, third, *backs)


def solution(mesh):
    bands = mesh.shape["lon"]
    placed = (
        P(None, ("lon", "lat"), None),
        P(None, ("lon", "lat"), None),
        P(None, ("lon", "lat")),
        P(),
        P(),
        P(),
    )

    def step(*args):
        return tuple(on_device(bands, *args))

    return jax.shard_map(
        step,
        mesh=mesh,
        in_specs=placed,
        out_specs=(P(None, ("lon", "lat"), None), P(("lon", "lat"), None)),
        check_vma=False,
    )
```

```python
import functools

import jax
import jax.numpy as jnp
from jax import lax
from jax.experimental import pallas as pl
from jax.experimental.pallas import tpu as pltpu
from jax.sharding import PartitionSpec as P

LEAF = 16
TASKS = 3
NBR = 4
NF = 32
W = 128
SLOTS = 8
SHIP = SLOTS - TASKS
ROWS = NBR * NF + 24
MASKS = (7, 5, 4, 3, 1)
F32 = jnp.float32

VMEM = pl.BlockSpec(memory_space=pltpu.VMEM)
SMEM = pl.BlockSpec(memory_space=pltpu.SMEM)


def params():
    return pltpu.CompilerParams(vmem_limit_bytes=40 * 2**20)


BF16 = jnp.bfloat16


def dot(a, b, across):
    return lax.dot_general(
        a, b, (((1,), (1 if across else 0,)), ((), ())), preferred_element_type=F32
    )


def thirds(a):
    high = a.astype(BF16)
    gap = a - high.astype(F32)
    middle = gap.astype(BF16)
    return high, middle, (gap - middle.astype(F32)).astype(BF16)


def halves(a):
    high = a.astype(BF16)
    return high, (a - high.astype(F32)).astype(BF16)


def six(a, b, across):
    a1, a2, a3 = a
    b1, b2, b3 = b
    return dot(
        jnp.concatenate([a3, a1, a2, a2, a1, a1], 1),
        jnp.concatenate([b1, b3, b2, b1, b2, b1], 1 if across else 0),
        across,
    )


def turned(a, b):
    a1, a2, a3 = thirds(a)
    b1, b2, b3 = thirds(b)
    return lax.dot_general(
        jnp.concatenate([a3, a1, a2, a2, a1, a1], 0),
        jnp.concatenate([b1, b3, b2, b1, b2, b1], 0),
        (((0,), (0,)), ((), ())),
        preferred_element_type=F32,
    )


def mm(a, b):
    return six(thirds(a), thirds(b), False)


def mmt(a, b):
    return six(thirds(a), thirds(b), True)


def mm3t(a, b):
    (a1, a2), (b1, b2) = halves(a), halves(b)
    return dot(jnp.concatenate([a2, a1, a1], 1), jnp.concatenate([b1, b2, b1], 1), True)


def mm3(a, b):
    (a1, a2), (b1, b2) = halves(a), halves(b)
    return dot(jnp.concatenate([a2, a1, a1], 1), jnp.concatenate([b1, b2, b1], 0), False)


def stack(*parts):
    return jnp.concatenate([x for x in parts if x.shape[0]], 0)


def sweeps(panels, off, tick):
    half = LEAF // 2
    down = lax.broadcasted_iota(jnp.int32, (half, W), 0)
    lane = lax.broadcasted_iota(jnp.int32, (half, W), 1)
    pairs = [[p[:half], p[half:]] for p in panels]

    def spread(x, at):
        return [jnp.broadcast_to(x[:, at + c : at + c + 1], (half, W)) for c in range(half)]

    for h in range(2):
        at = off + half * h
        inside = (lane >= at) & (lane < at + half)
        cols = [spread(p[h], at) for p in pairs]
        far = [spread(p[1 - h], at) for p in pairs]
        mine = [jnp.where(inside, jnp.where(lane == down + at, 1.0, 0.0), p[h]) for p in pairs]
        for i in range(0, half, 2):
            for s, col in enumerate(cols):
                p, q, r = (
                    jnp.broadcast_to(col[c][k : k + 1], (half, W))
                    for c, k in ((i, i), (i + 1, i), (i + 1, i + 1))
                )
                over = 1.0 / (p * r - q * q)
                x = jnp.where(down == i, col[i] - 1.0, col[i])
                y = jnp.where(down == i + 1, col[i + 1] - 1.0, col[i + 1])
                x, y = r * x - q * y, p * y - q * x
                for c in range(i + 2, min(i + 4, half)):
                    ahead = x * jnp.broadcast_to(col[c][i : i + 1], (half, W)) + y * jnp.broadcast_to(
                        col[c][i + 1 : i + 2], (half, W)
                    )
                    col[c] = col[c] - over * ahead
                x, y = over * x, over * y
                mine[s] = mine[s] - (
                    x * jnp.broadcast_to(mine[s][i : i + 1], (half, W))
                    + y * jnp.broadcast_to(mine[s][i + 1 : i + 2], (half, W))
                )
                for c in range(i + 4, half):
                    col[c] = col[c] - (
                        x * jnp.broadcast_to(col[c][i : i + 1], (half, W))
                        + y * jnp.broadcast_to(col[c][i + 1 : i + 2], (half, W))
                    )
            tick()
            tick()
        for s, p in enumerate(pairs):
            own = mine[s]
            gone = total_of(
                [far[s][c] * jnp.broadcast_to(own[c : c + 1], (half, W)) for c in range(half)]
            )
            p[h], p[1 - h] = own, jnp.where(inside, 0.0, p[1 - h]) - gone
    return [jnp.concatenate(p, 0) for p in pairs]


def total_of(terms):
    while len(terms) > 1:
        terms = [sum(terms[k : k + 2][1:], terms[k]) for k in range(0, len(terms), 2)]
    return terms[0]


def invert(tiles, behind):
    along = lax.broadcasted_iota(jnp.int32, (W, W), 1)
    state = {"ticks": 0, "done": 0}

    def tick():
        state["ticks"] += 1
        while state["done"] * W < state["ticks"] * len(behind):
            behind[state["done"]]()
            state["done"] += 1

    for off in range(0, W, LEAF):
        end = off + LEAF
        swept = sweeps([t[off:end] for t in tiles], off, tick)
        new = []
        in_cols = (along >= off) & (along < end)
        swept_lanes = along[:LEAF] < off
        for t, q in zip(tiles, swept):
            u = jnp.where(in_cols, 0.0, t) - turned(jnp.where(swept_lanes, -t[off:end], t[off:end]), q)
            new.append(stack(u[:off], q, u[end:]))
        tiles = new
    return tiles


def pool_row(block, my_band, my_sub, bands):
    band = block // (2 * SLOTS)
    sub = (block // SLOTS) % 2
    side = (band - my_band + 1 + bands) % bands
    flip = jnp.where(sub == my_sub, 0, 1)
    return (side * 2 + flip) * SLOTS + block % SLOTS


def join(points, values, other_points, other_values, pair):
    for k, (p, v) in enumerate(((points, values), (other_points, other_values))):
        pair[k, :3] = p[...]
        pair[k, 3:] = v[...]


def pack(bands, nb, *refs):
    pools, own, ships, pool = refs[:3], refs[3], refs[4:-1], refs[-1]
    band, sub = lax.axis_index("lon"), lax.axis_index("lat")
    for g in range(6):
        pool[:, g * SLOTS : (g + 1) * SLOTS, :] = pools[g // 2][g % 2]
    for s in range(SLOTS):
        dst = own.at[s] if s < TASKS else ships[s - TASKS]
        dst[NBR * NF :, :] = jnp.zeros((24, W), F32)
        for n in range(NBR):
            row = pool_row(nb[n, s], band, sub, bands)
            got = pool[:, pl.ds(row, 1), :].reshape(NF + 3, W)
            dst[n * NF : (n + 1) * NF, :] = got[3:]
            for d in range(3):
                dst[NBR * NF + 8 * d + n : NBR * NF + 8 * d + n + 1, :] = got[d : d + 1]
        for d in range(3):
            at = NBR * NF + 8 * d + NBR
            dst[at : at + 1, :] = pools[1][0, d, s : s + 1, :]


def solve(bands, counts, scale, nugget, own, *refs):
    ships, kept, sent, work, tiles, diag, left = refs[:SHIP], *refs[SHIP:]
    band, sub = lax.axis_index("lon"), lax.axis_index("lat")
    apart = bands // SLOTS
    work[...] = own[...]
    for k, mask in enumerate(MASKS):

        @pl.when(counts[(band ^ (mask * apart)) * 2 + sub] > TASKS - 1)
        def _():
            work[TASKS - 1] = ships[k][...]

    down = lax.broadcasted_iota(jnp.int32, (W, W), 0)
    along = lax.broadcasted_iota(jnp.int32, (W, W), 1)
    minus = jnp.full((W, W), -1.4426950408889634, F32) / scale[0]
    noise = jnp.where(down == along, nugget[0], 0.0)
    ones = jnp.ones((8, W), F32)

    def result(s):
        return sent if s == TASKS - 1 else kept.at[s]

    points = {}

    def build(s, a):
        if s not in points:
            rows = [work[s, NBR * NF + 8 * d : NBR * NF + 8 * d + 8, :] for d in range(3)]
            points[s] = rows, [r.T for r in rows]
        rows, cols = points[s]
        mine = [jnp.broadcast_to(c[:, a : a + 1], (W, W)) for c in cols]
        for b in range(min(a, NBR - 1) + 1):
            total = None
            for d in range(3):
                gap = mine[d] - jnp.broadcast_to(rows[d][b : b + 1], (W, W))
                total = gap * gap if total is None else total + gap * gap
            value = jnp.exp2(total * lax.rsqrt(jnp.maximum(total, 1e-30)) * minus)
            tiles[s, a, b] = value + noise if a == b else value

    def rows_of(s, b, low):
        return stack(
            tiles[s, low:, b].reshape((NBR + 1 - low) * W, W), work[s, b * NF : (b + 1) * NF, :]
        )

    def factor(s, j, given):
        g = diag[j % 2, s]
        left = mm3(given, g)
        return left + mm3(given - mm(left, tiles[s, j, j]), g)

    def near(s, j):
        given = tiles[s, j + 1, j]
        v = mm3(given, diag[j % 2, s])
        gap = given - mm(v, tiles[s, j, j])
        tiles[s, j + 1, j + 1] -= mmt(v, given) + mm3t(gap, v)

    def rest(s, j):
        low = j + 2 if j + 1 < NBR else NBR
        given = rows_of(s, j, low)
        v = factor(s, j, given)
        left[s, : v.shape[0]] = v
        result(s)[NF:] -= mmt(ones, v[-W - NF : -NF] * tiles[s, NBR, j])
        result(s)[:NF] += mmt(v[-NF:], tiles[s, NBR, j])

    def update(s, j, b):
        low = max(b, j + 2)
        size = (NBR + 1 - low) * W
        start = (low - (j + 2)) * W
        fresh = mmt(left[s, start : start + size + NF], tiles[s, b, j])
        tiles[s, low:, b] -= fresh[:size].reshape(NBR + 1 - low, W, W)
        work[s, b * NF : (b + 1) * NF, :] -= fresh[size:]

    tasks = range(TASKS)
    for s in tasks:
        result(s)[:NF] = jnp.zeros((NF, W), F32)
        result(s)[NF:] = ones
        build(s, 0)
    behind = [functools.partial(build, s, a) for a in range(1, NBR + 1) for s in tasks]
    for j in range(NBR):
        for s, g in enumerate(invert([tiles[s, j, j] for s in tasks], behind)):
            diag[j % 2, s] = g
        if j + 1 < NBR:
            for s in tasks:
                near(s, j)
            behind = [functools.partial(rest, s, j) for s in tasks]
            behind += [functools.partial(update, s, j, b) for b in range(j + 1, NBR) for s in tasks]
        else:
            for s in tasks:
                rest(s, j)


def assemble(bands, counts, kept, third, *refs):
    backs, predicted, variance = refs[:SHIP], refs[SHIP], refs[SHIP + 1]
    band, sub = lax.axis_index("lon"), lax.axis_index("lat")
    alive = counts[band * 2 + sub]
    for s in range(SLOTS):
        src = kept[s] if s < TASKS - 1 else third[...] if s < TASKS else backs[s - TASKS][...]
        src = jnp.where(s < alive, src, 0.0)
        predicted[:, s : s + 1, :] = src[:NF].reshape(NF, 1, W)
        variance[s : s + 1, :] = src[NF : NF + 1]


def arr(*shape):
    return jax.ShapeDtypeStruct(shape, F32)


def on_device(bands, coords, observed, neighbours, counts, lengthscale, nugget):
    axes = ("lon", "lat")
    total = bands * 2
    apart = bands // SLOTS

    def shift(x, lon, flip):
        pairs = [
            (l * 2 + h, ((l + lon) % bands) * 2 + (h ^ flip))
            for l in range(bands)
            for h in range(2)
        ]
        return lax.ppermute(x, axes, pairs)

    def trade(x, mask):
        pairs = [
            (l * 2 + h, (l ^ (mask * apart)) * 2 + h) for l in range(bands) for h in range(2)
        ]
        return lax.ppermute(x, axes, pairs)

    pair = pl.pallas_call(
        join,
        out_shape=arr(2, NF + 3, SLOTS, W),
        in_specs=[VMEM] * 4,
        out_specs=VMEM,
        compiler_params=params(),
        name="join",
    )(coords, observed, shift(coords, 0, 1), shift(observed, 0, 1))
    pool = [shift(pair, 1, 0), pair, shift(pair, -1, 0)]
    own, *out = pl.pallas_call(
        lambda *r: pack(bands, *r),
        out_shape=[arr(TASKS, ROWS, W)] + [arr(ROWS, W)] * SHIP,
        in_specs=[SMEM] + [VMEM] * 3,
        out_specs=[VMEM] * (1 + SHIP),
        scratch_shapes=[pltpu.VMEM((NF + 3, 6 * SLOTS, W), F32)],
        compiler_params=params(),
        name="pack",
    )(neighbours, *pool)
    ships = [trade(x, mask) for x, mask in zip(out, MASKS)]
    kept, third = pl.pallas_call(
        lambda *r: solve(bands, *r),
        out_shape=[arr(TASKS - 1, NF + 8, W), arr(NF + 8, W)],
        in_specs=[SMEM] * 3 + [VMEM] * (1 + SHIP),
        out_specs=[VMEM] * 2,
        scratch_shapes=[
            pltpu.VMEM((TASKS, ROWS, W), F32),
            pltpu.VMEM((TASKS, NBR + 1, NBR, W, W), F32),
            pltpu.VMEM((2, TASKS, W, W), F32),
            pltpu.VMEM((TASKS, (NBR - 1) * W + NF, W), F32),
        ],
        compiler_params=params(),
        name="solve",
    )(counts, lengthscale, nugget, own, *ships)
    backs = [trade(third, mask) for mask in reversed(MASKS)][::-1]
    return pl.pallas_call(
        lambda *r: assemble(bands, *r),
        out_shape=[arr(NF, SLOTS, W), arr(SLOTS, W)],
        in_specs=[SMEM] + [VMEM] * (2 + SHIP),
        out_specs=[VMEM] * 2,
        compiler_params=params(),
        name="assemble",
    )(counts, kept, third, *backs)


def solution(mesh):
    bands = mesh.shape["lon"]
    placed = (
        P(None, ("lon", "lat"), None),
        P(None, ("lon", "lat"), None),
        P(None, ("lon", "lat")),
        P(),
        P(),
        P(),
    )

    def step(*args):
        return tuple(on_device(bands, *args))

    return jax.shard_map(
        step,
        mesh=mesh,
        in_specs=placed,
        out_specs=(P(None, ("lon", "lat"), None), P(("lon", "lat"), None)),
        check_vma=False,
    )
```

```python
import functools

import jax
import jax.numpy as jnp
from jax import lax
from jax.experimental import pallas as pl
from jax.experimental.pallas import tpu as pltpu
from jax.sharding import PartitionSpec as P

LEAF = 16
TASKS = 3
NBR = 4
NF = 32
W = 128
SLOTS = 8
SHIP = SLOTS - TASKS
ROWS = NBR * NF + 24
MASKS = (7, 5, 4, 3, 1)
F32 = jnp.float32

VMEM = pl.BlockSpec(memory_space=pltpu.VMEM)
SMEM = pl.BlockSpec(memory_space=pltpu.SMEM)


def params():
    return pltpu.CompilerParams(vmem_limit_bytes=40 * 2**20)


BF16 = jnp.bfloat16


def dot(a, b, across):
    return lax.dot_general(
        a, b, (((1,), (1 if across else 0,)), ((), ())), preferred_element_type=F32
    )


def thirds(a):
    high = a.astype(BF16)
    gap = a - high.astype(F32)
    middle = gap.astype(BF16)
    return high, middle, (gap - middle.astype(F32)).astype(BF16)


def halves(a):
    high = a.astype(BF16)
    return high, (a - high.astype(F32)).astype(BF16)


def six(a, b, across):
    a1, a2, a3 = a
    b1, b2, b3 = b
    return dot(
        jnp.concatenate([a3, a1, a2, a2, a1, a1], 1),
        jnp.concatenate([b1, b3, b2, b1, b2, b1], 1 if across else 0),
        across,
    )


def turned(a, b):
    a1, a2, a3 = thirds(a)
    b1, b2, b3 = thirds(b)
    return lax.dot_general(
        jnp.concatenate([a3, a1, a2, a2, a1, a1], 0),
        jnp.concatenate([b1, b3, b2, b1, b2, b1], 0),
        (((0,), (0,)), ((), ())),
        preferred_element_type=F32,
    )


def mm(a, b):
    return six(thirds(a), thirds(b), False)


def mmt(a, b):
    return six(thirds(a), thirds(b), True)


def mm3t(a, b):
    (a1, a2), (b1, b2) = halves(a), halves(b)
    return dot(jnp.concatenate([a2, a1, a1], 1), jnp.concatenate([b1, b2, b1], 1), True)


def mm3(a, b):
    (a1, a2), (b1, b2) = halves(a), halves(b)
    return dot(jnp.concatenate([a2, a1, a1], 1), jnp.concatenate([b1, b2, b1], 0), False)


def stack(*parts):
    return jnp.concatenate([x for x in parts if x.shape[0]], 0)


def sweeps(panels, off, tick):
    half = LEAF // 2
    down = lax.broadcasted_iota(jnp.int32, (half, W), 0)
    lane = lax.broadcasted_iota(jnp.int32, (half, W), 1)
    pairs = [[p[:half], p[half:]] for p in panels]

    def spread(x, at):
        return [jnp.broadcast_to(x[:, at + c : at + c + 1], (half, W)) for c in range(half)]

    for h in range(2):
        at = off + half * h
        inside = (lane >= at) & (lane < at + half)
        cols = [spread(p[h], at) for p in pairs]
        far = [spread(p[1 - h], at) for p in pairs]
        mine = [jnp.where(inside, jnp.where(lane == down + at, 1.0, 0.0), p[h]) for p in pairs]
        for i in range(0, half, 2):
            for s, col in enumerate(cols):
                p, q, r = (
                    jnp.broadcast_to(col[c][k : k + 1], (half, W))
                    for c, k in ((i, i), (i + 1, i), (i + 1, i + 1))
                )
                over = 1.0 / (p * r - q * q)
                x = jnp.where(down == i, col[i] - 1.0, col[i])
                y = jnp.where(down == i + 1, col[i + 1] - 1.0, col[i + 1])
                x, y = r * x - q * y, p * y - q * x
                for c in range(i + 2, min(i + 4, half)):
                    ahead = x * jnp.broadcast_to(col[c][i : i + 1], (half, W)) + y * jnp.broadcast_to(
                        col[c][i + 1 : i + 2], (half, W)
                    )
                    col[c] = col[c] - over * ahead
                x, y = over * x, over * y
                mine[s] = mine[s] - (
                    x * jnp.broadcast_to(mine[s][i : i + 1], (half, W))
                    + y * jnp.broadcast_to(mine[s][i + 1 : i + 2], (half, W))
                )
                for c in range(i + 4, half):
                    col[c] = col[c] - (
                        x * jnp.broadcast_to(col[c][i : i + 1], (half, W))
                        + y * jnp.broadcast_to(col[c][i + 1 : i + 2], (half, W))
                    )
            tick()
            tick()
        for s, p in enumerate(pairs):
            own = mine[s]
            gone = total_of(
                [far[s][c] * jnp.broadcast_to(own[c : c + 1], (half, W)) for c in range(half)]
            )
            p[h], p[1 - h] = own, jnp.where(inside, 0.0, p[1 - h]) - gone
    return [jnp.concatenate(p, 0) for p in pairs]


def total_of(terms):
    while len(terms) > 1:
        terms = [sum(terms[k : k + 2][1:], terms[k]) for k in range(0, len(terms), 2)]
    return terms[0]


def invert(tiles, behind):
    along = lax.broadcasted_iota(jnp.int32, (W, W), 1)
    state = {"ticks": 0, "done": 0}

    def tick():
        state["ticks"] += 1
        while state["done"] * W < state["ticks"] * len(behind):
            behind[state["done"]]()
            state["done"] += 1

    for off in range(0, W, LEAF):
        end = off + LEAF
        swept = sweeps([t[off:end] for t in tiles], off, tick)
        new = []
        in_cols = (along >= off) & (along < end)
        swept_lanes = along[:LEAF] < off
        for t, q in zip(tiles, swept):
            u = jnp.where(in_cols, 0.0, t) - turned(jnp.where(swept_lanes, -t[off:end], t[off:end]), q)
            new.append(stack(u[:off], q, u[end:]))
        tiles = new
    return tiles


def pool_row(block, my_band, my_sub, bands):
    band = block // (2 * SLOTS)
    sub = (block // SLOTS) % 2
    side = (band - my_band + 1 + bands) % bands
    side = jnp.where(my_band % 2 == 1, side, 2 - side)
    flip = jnp.where(sub == my_sub, 0, 1)
    return (side * 2 + flip) * SLOTS + block % SLOTS


def pack(bands, nb, *refs):
    pools, own, ships, pool = refs[:6], refs[6], refs[7:-1], refs[-1]
    band, sub = lax.axis_index("lon"), lax.axis_index("lat")
    for g in range(6):
        pool[:, g * SLOTS : (g + 1) * SLOTS, :] = pools[g][...]
    for s in range(SLOTS):
        dst = own.at[s] if s < TASKS else ships[s - TASKS]
        dst[NBR * NF :, :] = jnp.zeros((24, W), F32)
        for n in range(NBR):
            row = pool_row(nb[n, s], band, sub, bands)
            got = pool[:, pl.ds(row, 1), :].reshape(NF + 3, W)
            dst[n * NF : (n + 1) * NF, :] = got[3:]
            for d in range(3):
                dst[NBR * NF + 8 * d + n : NBR * NF + 8 * d + n + 1, :] = got[d : d + 1]
        for d in range(3):
            at = NBR * NF + 8 * d + NBR
            dst[at : at + 1, :] = pools[2][d, s : s + 1, :]


def solve(bands, counts, scale, nugget, own, *refs):
    ships, kept, sent, work, tiles, diag, left = refs[:SHIP], *refs[SHIP:]
    band, sub = lax.axis_index("lon"), lax.axis_index("lat")
    apart = bands // SLOTS
    work[...] = own[...]
    for k, mask in enumerate(MASKS):

        @pl.when(counts[(band ^ (mask * apart)) * 2 + sub] > TASKS - 1)
        def _():
            work[TASKS - 1] = ships[k][...]

    down = lax.broadcasted_iota(jnp.int32, (W, W), 0)
    along = lax.broadcasted_iota(jnp.int32, (W, W), 1)
    minus = jnp.full((W, W), -1.4426950408889634, F32) / scale[0]
    noise = jnp.where(down == along, nugget[0], 0.0)
    ones = jnp.ones((8, W), F32)

    def result(s):
        return sent if s == TASKS - 1 else kept.at[s]

    points = {}

    def build(s, a):
        if s not in points:
            rows = [work[s, NBR * NF + 8 * d : NBR * NF + 8 * d + 8, :] for d in range(3)]
            points[s] = rows, [r.T for r in rows]
        rows, cols = points[s]
        mine = [jnp.broadcast_to(c[:, a : a + 1], (W, W)) for c in cols]
        for b in range(min(a, NBR - 1) + 1):
            total = None
            for d in range(3):
                gap = mine[d] - jnp.broadcast_to(rows[d][b : b + 1], (W, W))
                total = gap * gap if total is None else total + gap * gap
            value = jnp.exp2(total * lax.rsqrt(jnp.maximum(total, 1e-30)) * minus)
            tiles[s, a, b] = value + noise if a == b else value

    def rows_of(s, b, low):
        return stack(
            tiles[s, low:, b].reshape((NBR + 1 - low) * W, W), work[s, b * NF : (b + 1) * NF, :]
        )

    def factor(s, j, given):
        g = diag[j % 2, s]
        left = mm3(given, g)
        return left + mm3(given - mm(left, tiles[s, j, j]), g)

    def near(s, j):
        given = tiles[s, j + 1, j]
        v = mm3(given, diag[j % 2, s])
        gap = given - mm(v, tiles[s, j, j])
        tiles[s, j + 1, j + 1] -= mmt(v, given) + mm3t(gap, v)

    def rest(s, j):
        low = j + 2 if j + 1 < NBR else NBR
        given = rows_of(s, j, low)
        v = factor(s, j, given)
        left[s, : v.shape[0]] = v
        result(s)[NF:] -= mmt(ones, v[-W - NF : -NF] * tiles[s, NBR, j])
        result(s)[:NF] += mmt(v[-NF:], tiles[s, NBR, j])

    def update(s, j, b):
        low = max(b, j + 2)
        size = (NBR + 1 - low) * W
        start = (low - (j + 2)) * W
        fresh = mmt(left[s, start : start + size + NF], tiles[s, b, j])
        tiles[s, low:, b] -= fresh[:size].reshape(NBR + 1 - low, W, W)
        work[s, b * NF : (b + 1) * NF, :] -= fresh[size:]

    tasks = range(TASKS)
    for s in tasks:
        result(s)[:NF] = jnp.zeros((NF, W), F32)
        result(s)[NF:] = ones
        build(s, 0)
    behind = [functools.partial(build, s, a) for a in range(1, NBR + 1) for s in tasks]
    for j in range(NBR):
        for s, g in enumerate(invert([tiles[s, j, j] for s in tasks], behind)):
            diag[j % 2, s] = g
        if j + 1 < NBR:
            for s in tasks:
                near(s, j)
            behind = [functools.partial(rest, s, j) for s in tasks]
            behind += [functools.partial(update, s, j, b) for b in range(j + 1, NBR) for s in tasks]
        else:
            for s in tasks:
                rest(s, j)


def assemble(bands, counts, kept, third, *refs):
    backs, predicted, variance = refs[:SHIP], refs[SHIP], refs[SHIP + 1]
    band, sub = lax.axis_index("lon"), lax.axis_index("lat")
    alive = counts[band * 2 + sub]
    for s in range(SLOTS):
        src = kept[s] if s < TASKS - 1 else third[...] if s < TASKS else backs[s - TASKS][...]
        src = jnp.where(s < alive, src, 0.0)
        predicted[:, s : s + 1, :] = src[:NF].reshape(NF, 1, W)
        variance[s : s + 1, :] = src[NF : NF + 1]


def arr(*shape):
    return jax.ShapeDtypeStruct(shape, F32)


def on_device(bands, coords, observed, neighbours, counts, lengthscale, nugget):
    axes = ("lon", "lat")
    total = bands * 2
    apart = bands // SLOTS

    def shift(x, lon, flip):
        pairs = [
            (l * 2 + h, ((l + lon) % bands) * 2 + (h ^ flip))
            for l in range(bands)
            for h in range(2)
        ]
        return lax.ppermute(x, axes, pairs)

    def swap(x, odd):
        pairs = [
            (l * 2 + h, (((l + odd) ^ 1) - odd) % bands * 2 + h) for l in range(bands) for h in range(2)
        ]
        return lax.ppermute(x, axes, pairs)

    def pool_of(x):
        other = shift(x, 0, 1)
        chip, far = swap(x, 0), swap(x, 1)
        return [chip, swap(other, 0), x, other, far, swap(other, 1)]

    def trade(x, mask):
        pairs = [
            (l * 2 + h, (l ^ (mask * apart)) * 2 + h) for l in range(bands) for h in range(2)
        ]
        return lax.ppermute(x, axes, pairs)

    pool = pool_of(jnp.concatenate([coords, observed], axis=0))
    own, *out = pl.pallas_call(
        lambda *r: pack(bands, *r),
        out_shape=[arr(TASKS, ROWS, W)] + [arr(ROWS, W)] * SHIP,
        in_specs=[SMEM] + [VMEM] * 6,
        out_specs=[VMEM] * (1 + SHIP),
        scratch_shapes=[pltpu.VMEM((NF + 3, 6 * SLOTS, W), F32)],
        compiler_params=params(),
        name="pack",
    )(neighbours, *pool)
    ships = [trade(x, mask) for x, mask in zip(out, MASKS)]
    kept, third = pl.pallas_call(
        lambda *r: solve(bands, *r),
        out_shape=[arr(TASKS - 1, NF + 8, W), arr(NF + 8, W)],
        in_specs=[SMEM] * 3 + [VMEM] * (1 + SHIP),
        out_specs=[VMEM] * 2,
        scratch_shapes=[
            pltpu.VMEM((TASKS, ROWS, W), F32),
            pltpu.VMEM((TASKS, NBR + 1, NBR, W, W), F32),
            pltpu.VMEM((2, TASKS, W, W), F32),
            pltpu.VMEM((TASKS, (NBR - 1) * W + NF, W), F32),
        ],
        compiler_params=params(),
        name="solve",
    )(counts, lengthscale, nugget, own, *ships)
    backs = [trade(third, mask) for mask in MASKS]
    return pl.pallas_call(
        lambda *r: assemble(bands, *r),
        out_shape=[arr(NF, SLOTS, W), arr(SLOTS, W)],
        in_specs=[SMEM] + [VMEM] * (2 + SHIP),
        out_specs=[VMEM] * 2,
        compiler_params=params(),
        name="assemble",
    )(counts, kept, third, *backs)


def solution(mesh):
    bands = mesh.shape["lon"]
    placed = (
        P(None, ("lon", "lat"), None),
        P(None, ("lon", "lat"), None),
        P(None, ("lon", "lat")),
        P(),
        P(),
        P(),
    )

    def step(*args):
        return tuple(on_device(bands, *args))

    return jax.shard_map(
        step,
        mesh=mesh,
        in_specs=placed,
        out_specs=(P(None, ("lon", "lat"), None), P(("lon", "lat"), None)),
        check_vma=False,
    )
```

```python
import functools

import jax
import jax.numpy as jnp
from jax import lax
from jax.experimental import pallas as pl
from jax.experimental.pallas import tpu as pltpu
from jax.sharding import PartitionSpec as P

LEAF = 16
TASKS = 3
NBR = 4
NF = 32
W = 128
SLOTS = 8
SHIP = SLOTS - TASKS
ROWS = NBR * NF + 24
MASKS = (7, 5, 4, 3, 1)
F32 = jnp.float32

VMEM = pl.BlockSpec(memory_space=pltpu.VMEM)
SMEM = pl.BlockSpec(memory_space=pltpu.SMEM)


def params():
    return pltpu.CompilerParams(vmem_limit_bytes=40 * 2**20)


BF16 = jnp.bfloat16


def dot(a, b, across):
    return lax.dot_general(
        a, b, (((1,), (1 if across else 0,)), ((), ())), preferred_element_type=F32
    )


def thirds(a):
    high = a.astype(BF16)
    gap = a - high.astype(F32)
    middle = gap.astype(BF16)
    return high, middle, (gap - middle.astype(F32)).astype(BF16)


def halves(a):
    high = a.astype(BF16)
    return high, (a - high.astype(F32)).astype(BF16)


def six(a, b, across):
    a1, a2, a3 = a
    b1, b2, b3 = b
    return dot(
        jnp.concatenate([a3, a1, a2, a2, a1, a1], 1),
        jnp.concatenate([b1, b3, b2, b1, b2, b1], 1 if across else 0),
        across,
    )


def turned(a, b):
    a1, a2, a3 = thirds(a)
    b1, b2, b3 = thirds(b)
    return lax.dot_general(
        jnp.concatenate([a3, a1, a2, a2, a1, a1], 0),
        jnp.concatenate([b1, b3, b2, b1, b2, b1], 0),
        (((0,), (0,)), ((), ())),
        preferred_element_type=F32,
    )


def mm(a, b):
    return six(thirds(a), thirds(b), False)


def mmt(a, b):
    return six(thirds(a), thirds(b), True)


def mm3t(a, b):
    (a1, a2), (b1, b2) = halves(a), halves(b)
    return dot(jnp.concatenate([a2, a1, a1], 1), jnp.concatenate([b1, b2, b1], 1), True)


def mm3(a, b):
    (a1, a2), (b1, b2) = halves(a), halves(b)
    return dot(jnp.concatenate([a2, a1, a1], 1), jnp.concatenate([b1, b2, b1], 0), False)


def stack(*parts):
    return jnp.concatenate([x for x in parts if x.shape[0]], 0)


def sweeps(panels, off, tick):
    half = LEAF // 2
    down = lax.broadcasted_iota(jnp.int32, (half, W), 0)
    lane = lax.broadcasted_iota(jnp.int32, (half, W), 1)
    pairs = [[p[:half], p[half:]] for p in panels]

    def spread(x, at):
        return [jnp.broadcast_to(x[:, at + c : at + c + 1], (half, W)) for c in range(half)]

    for h in range(2):
        at = off + half * h
        inside = (lane >= at) & (lane < at + half)
        cols = [spread(p[h], at) for p in pairs]
        far = [spread(p[1 - h], at) for p in pairs]
        mine = [jnp.where(inside, jnp.where(lane == down + at, 1.0, 0.0), p[h]) for p in pairs]
        for i in range(0, half, 2):
            for s, col in enumerate(cols):
                p, q, r = (
                    jnp.broadcast_to(col[c][k : k + 1], (half, W))
                    for c, k in ((i, i), (i + 1, i), (i + 1, i + 1))
                )
                over = 1.0 / (p * r - q * q)
                x = jnp.where(down == i, col[i] - 1.0, col[i])
                y = jnp.where(down == i + 1, col[i + 1] - 1.0, col[i + 1])
                x, y = r * x - q * y, p * y - q * x
                for c in range(i + 2, min(i + 4, half)):
                    ahead = x * jnp.broadcast_to(col[c][i : i + 1], (half, W)) + y * jnp.broadcast_to(
                        col[c][i + 1 : i + 2], (half, W)
                    )
                    col[c] = col[c] - over * ahead
                x, y = over * x, over * y
                mine[s] = mine[s] - (
                    x * jnp.broadcast_to(mine[s][i : i + 1], (half, W))
                    + y * jnp.broadcast_to(mine[s][i + 1 : i + 2], (half, W))
                )
                for c in range(i + 4, half):
                    col[c] = col[c] - (
                        x * jnp.broadcast_to(col[c][i : i + 1], (half, W))
                        + y * jnp.broadcast_to(col[c][i + 1 : i + 2], (half, W))
                    )
            tick()
            tick()
        for s, p in enumerate(pairs):
            own = mine[s]
            gone = total_of(
                [far[s][c] * jnp.broadcast_to(own[c : c + 1], (half, W)) for c in range(half)]
            )
            p[h], p[1 - h] = own, jnp.where(inside, 0.0, p[1 - h]) - gone
    return [jnp.concatenate(p, 0) for p in pairs]


def total_of(terms):
    while len(terms) > 1:
        terms = [sum(terms[k : k + 2][1:], terms[k]) for k in range(0, len(terms), 2)]
    return terms[0]


def invert(tiles, behind):
    along = lax.broadcasted_iota(jnp.int32, (W, W), 1)
    state = {"ticks": 0, "done": 0}

    def tick():
        state["ticks"] += 1
        while state["done"] * W < state["ticks"] * len(behind):
            behind[state["done"]]()
            state["done"] += 1

    for off in range(0, W, LEAF):
        end = off + LEAF
        swept = sweeps([t[off:end] for t in tiles], off, tick)
        new = []
        in_cols = (along >= off) & (along < end)
        swept_lanes = along[:LEAF] < off
        for t, q in zip(tiles, swept):
            u = jnp.where(in_cols, 0.0, t) - turned(jnp.where(swept_lanes, -t[off:end], t[off:end]), q)
            new.append(stack(u[:off], q, u[end:]))
        tiles = new
    return tiles


def pool_row(block, my_band, my_sub, bands):
    band = block // (2 * SLOTS)
    sub = (block // SLOTS) % 2
    side = (band - my_band + 1 + bands) % bands
    flip = jnp.where(sub == my_sub, 0, 1)
    return (side * 2 + flip) * SLOTS + block % SLOTS


def pack(bands, nb, *refs):
    pools, own, ships, pool = refs[:6], refs[6], refs[7:-1], refs[-1]
    band, sub = lax.axis_index("lon"), lax.axis_index("lat")
    for g in range(6):
        pool[:, g * SLOTS : (g + 1) * SLOTS, :] = pools[g][...]
    for s in range(SLOTS):
        dst = own.at[s] if s < TASKS else ships[s - TASKS]
        dst[NBR * NF :, :] = jnp.zeros((24, W), F32)
        for n in range(NBR):
            row = pool_row(nb[n, s], band, sub, bands)
            got = pool[:, pl.ds(row, 1), :].reshape(NF + 3, W)
            dst[n * NF : (n + 1) * NF, :] = got[3:]
            for d in range(3):
                dst[NBR * NF + 8 * d + n : NBR * NF + 8 * d + n + 1, :] = got[d : d + 1]
        for d in range(3):
            at = NBR * NF + 8 * d + NBR
            dst[at : at + 1, :] = pools[2][d, s : s + 1, :]


def solve(bands, counts, scale, nugget, own, *refs):
    ships, kept, sent, work, tiles, diag, left = refs[:SHIP], *refs[SHIP:]
    band, sub = lax.axis_index("lon"), lax.axis_index("lat")
    apart = bands // SLOTS
    work[...] = own[...]
    for k, mask in enumerate(MASKS):

        @pl.when(counts[(band ^ (mask * apart)) * 2 + sub] > TASKS - 1)
        def _():
            work[TASKS - 1] = ships[k][...]

    down = lax.broadcasted_iota(jnp.int32, (W, W), 0)
    along = lax.broadcasted_iota(jnp.int32, (W, W), 1)
    minus = jnp.full((W, W), -1.4426950408889634, F32) / scale[0]
    noise = jnp.where(down == along, nugget[0], 0.0)
    ones = jnp.ones((8, W), F32)

    def result(s):
        return sent if s == TASKS - 1 else kept.at[s]

    points = {}

    def build(s, a):
        if s not in points:
            rows = [work[s, NBR * NF + 8 * d : NBR * NF + 8 * d + 8, :] for d in range(3)]
            points[s] = rows, [r.T for r in rows]
        rows, cols = points[s]
        mine = [jnp.broadcast_to(c[:, a : a + 1], (W, W)) for c in cols]
        for b in range(min(a, NBR - 1) + 1):
            total = None
            for d in range(3):
                gap = mine[d] - jnp.broadcast_to(rows[d][b : b + 1], (W, W))
                total = gap * gap if total is None else total + gap * gap
            value = jnp.exp2(total * lax.rsqrt(jnp.maximum(total, 1e-30)) * minus)
            tiles[s, a, b] = value + noise if a == b else value

    def rows_of(s, b, low):
        return stack(
            tiles[s, low:, b].reshape((NBR + 1 - low) * W, W), work[s, b * NF : (b + 1) * NF, :]
        )

    def factor(s, j, given):
        g = diag[j % 2, s]
        left = mm3(given, g)
        return left + mm3(given - mm(left, tiles[s, j, j]), g)

    def near(s, j):
        given = tiles[s, j + 1, j]
        v = mm3(given, diag[j % 2, s])
        gap = given - mm(v, tiles[s, j, j])
        tiles[s, j + 1, j + 1] -= mmt(v, given) + mm3t(gap, v)

    def rest(s, j):
        low = j + 2 if j + 1 < NBR else NBR
        given = rows_of(s, j, low)
        v = factor(s, j, given)
        left[s, : v.shape[0]] = v
        result(s)[NF:] -= mmt(ones, v[-W - NF : -NF] * tiles[s, NBR, j])
        result(s)[:NF] += mmt(v[-NF:], tiles[s, NBR, j])

    def update(s, j, b):
        low = max(b, j + 2)
        size = (NBR + 1 - low) * W
        start = (low - (j + 2)) * W
        fresh = mmt(left[s, start : start + size + NF], tiles[s, b, j])
        tiles[s, low:, b] -= fresh[:size].reshape(NBR + 1 - low, W, W)
        work[s, b * NF : (b + 1) * NF, :] -= fresh[size:]

    tasks = range(TASKS)
    for s in tasks:
        result(s)[:NF] = jnp.zeros((NF, W), F32)
        result(s)[NF:] = ones
        build(s, 0)
    behind = [functools.partial(build, s, a) for a in range(1, NBR + 1) for s in tasks]
    for j in range(NBR):
        for s, g in enumerate(invert([tiles[s, j, j] for s in tasks], behind)):
            diag[j % 2, s] = g
        if j + 1 < NBR:
            for s in tasks:
                near(s, j)
            behind = [functools.partial(rest, s, j) for s in tasks]
            behind += [functools.partial(update, s, j, b) for b in range(j + 1, NBR) for s in tasks]
        else:
            for s in tasks:
                rest(s, j)


def assemble(bands, counts, kept, third, *refs):
    backs, predicted, variance = refs[:SHIP], refs[SHIP], refs[SHIP + 1]
    band, sub = lax.axis_index("lon"), lax.axis_index("lat")
    alive = counts[band * 2 + sub]
    for s in range(SLOTS):
        src = kept[s] if s < TASKS - 1 else third[...] if s < TASKS else backs[s - TASKS][...]
        src = jnp.where(s < alive, src, 0.0)
        predicted[:, s : s + 1, :] = src[:NF].reshape(NF, 1, W)
        variance[s : s + 1, :] = src[NF : NF + 1]


def arr(*shape):
    return jax.ShapeDtypeStruct(shape, F32)


def on_device(bands, coords, observed, neighbours, counts, lengthscale, nugget):
    axes = ("lon", "lat")
    total = bands * 2
    apart = bands // SLOTS

    def shift(x, lon, flip):
        pairs = [
            (l * 2 + h, ((l + lon) % bands) * 2 + (h ^ flip))
            for l in range(bands)
            for h in range(2)
        ]
        return lax.ppermute(x, axes, pairs)

    def pool_of(x):
        return [
            x if (away, flip) == (0, 0) else shift(x, -away, flip)
            for away in (-1, 0, 1)
            for flip in (0, 1)
        ]

    def trade(x, mask):
        pairs = [
            (l * 2 + h, (l ^ (mask * apart)) * 2 + h) for l in range(bands) for h in range(2)
        ]
        return lax.ppermute(x, axes, pairs)

    pool = pool_of(jnp.concatenate([coords, observed], axis=0))
    own, *out = pl.pallas_call(
        lambda *r: pack(bands, *r),
        out_shape=[arr(TASKS, ROWS, W)] + [arr(ROWS, W)] * SHIP,
        in_specs=[SMEM] + [VMEM] * 6,
        out_specs=[VMEM] * (1 + SHIP),
        scratch_shapes=[pltpu.VMEM((NF + 3, 6 * SLOTS, W), F32)],
        compiler_params=params(),
        name="pack",
    )(neighbours, *pool)
    ships = [trade(x, mask) for x, mask in zip(out, MASKS)]
    kept, third = pl.pallas_call(
        lambda *r: solve(bands, *r),
        out_shape=[arr(TASKS - 1, NF + 8, W), arr(NF + 8, W)],
        in_specs=[SMEM] * 3 + [VMEM] * (1 + SHIP),
        out_specs=[VMEM] * 2,
        scratch_shapes=[
            pltpu.VMEM((TASKS, ROWS, W), F32),
            pltpu.VMEM((TASKS, NBR + 1, NBR, W, W), F32),
            pltpu.VMEM((2, TASKS, W, W), F32),
            pltpu.VMEM((TASKS, (NBR - 1) * W + NF, W), F32),
        ],
        compiler_params=params(),
        name="solve",
    )(counts, lengthscale, nugget, own, *ships)
    backs = [trade(third, mask) for mask in MASKS]
    return pl.pallas_call(
        lambda *r: assemble(bands, *r),
        out_shape=[arr(NF, SLOTS, W), arr(SLOTS, W)],
        in_specs=[SMEM] + [VMEM] * (2 + SHIP),
        out_specs=[VMEM] * 2,
        compiler_params=params(),
        name="assemble",
    )(counts, kept, third, *backs)


def solution(mesh):
    bands = mesh.shape["lon"]
    placed = (
        P(None, ("lon", "lat"), None),
        P(None, ("lon", "lat"), None),
        P(None, ("lon", "lat")),
        P(),
        P(),
        P(),
    )

    def step(*args):
        return tuple(on_device(bands, *args))

    return jax.shard_map(
        step,
        mesh=mesh,
        in_specs=placed,
        out_specs=(P(None, ("lon", "lat"), None), P(("lon", "lat"), None)),
        check_vma=False,
    )
```
